256 devices in a mesh: clip: 16 (over z, x_hi), tm: 16 (over x_lo, y, core).
Axes of the slice: x: 4 (x_hi: 2, x_lo: 2; x = x_hi * 2 + x_lo), y: 4, z: 8, core: 2. Of those that a mesh axis runs over, the one named last changes fastest.
Arguments:
- queries: bfloat16 [16, 4096, 1536], P('clip', 'tm'), may hold values from -8 to 8
- key_rows: bfloat16 [16, 4096, 1536], P('clip', 'tm'), may hold values from -8 to 8
- value_rows: bfloat16 [16, 4096, 1536], P('clip', 'tm'), may hold values from -6 to 6
- grad_out: bfloat16 [16, 4096, 1536], P('clip', 'tm'), may hold values from -16 to 16
- query_gain: float32 [128], replicated, may hold values from 0.5 to 5
- key_gain: float32 [128], replicated, may hold values from 0.5 to 5
- valid_frames: int32 [16, 16], P('clip'), may hold values from 1 to 4
- window_start: int32 [16, 64], P('clip'), may hold values from 0 to 2
Outputs:
- attended: bfloat16 [16, 4096, 1536], P('clip', 'tm')
- query_grad: bfloat16 [16, 4096, 1536], P('clip', 'tm')
- key_grad: bfloat16 [16, 4096, 1536], P('clip', 'tm')
- value_grad: bfloat16 [16, 4096, 1536], P('clip', 'tm')
- query_gain_grad: float32 [128], replicated
- key_gain_grad: float32 [128], replicated
The draws below stay inside these ranges and needn't reach their ends.
All inputs are finite; a program needn't handle non-finite values.
Results may differ from the reference program's by a relative error of at most 0.0045.
The reference program's roundings to bfloat16 on the way count: a program that leaves them out, or rounds other values in their place, can miss the bound.
Values may be sent and summed in bfloat16 or wider, within the bound.
A program may use at most 128 MiB of HBM per device.

```python
import math
import jax
import jax.numpy as jnp
from jax import lax

H = 12
HD = 128
HH = 1536
TF = 4
TH = 4
TW = 4
TILE = 64
TT = 1
GH = 1
GW = 4
WW = 2
TILES_SLAB = 4
SLAB_TOK = 256
SLABS = 16
CLIPS = 16
TOKENS = 4096


def draw_queries(key, part):
    key = jax.random.fold_in(key, 1)
    first, second = jax.random.split(key, 2)
    shape = (CLIPS, TOKENS, H, HD)
    drawn = jax.random.normal(first, shape, jnp.float32)
    lifts = jnp.exp(jax.random.uniform(second, (CLIPS, TOKENS, H, 1), jnp.float32, -0.7, 1.4))
    base = jnp.clip(drawn * lifts, -8.0, 8.0)
    return base.reshape(CLIPS, TOKENS, H * HD).astype(jnp.bfloat16)


def draw_key_rows(key, part):
    key = jax.random.fold_in(key, 2)
    first, second = jax.random.split(key, 2)
    shape = (CLIPS, TOKENS, H, HD)
    drawn = jax.random.normal(first, shape, jnp.float32)
    lifts = jnp.exp(jax.random.uniform(second, (CLIPS, TOKENS, H, 1), jnp.float32, -0.7, 1.4))
    base = jnp.clip(drawn * lifts, -8.0, 8.0)
    return base.reshape(CLIPS, TOKENS, H * HD).astype(jnp.bfloat16)


def draw_query_gain(key, part):
    key = jax.random.fold_in(key, 3)
    return jax.random.uniform(key, (HD,), jnp.float32, 0.5, 2.0)


def draw_key_gain(key, part):
    key = jax.random.fold_in(key, 4)
    return jax.random.uniform(key, (HD,), jnp.float32, 0.5, 2.0)


def draw_grad_out(key, part):
    key = jax.random.fold_in(key, 5)
    clip_rise = 1.0 + 2.0 * jnp.arange(CLIPS).astype(jnp.float32) / max(CLIPS - 1, 1)
    slab_rise = 1.0 + 2.0 * (jnp.arange(TOKENS) // SLAB_TOK).astype(jnp.float32) / max(SLABS - 1, 1)
    rise = clip_rise[:, None, None] * slab_rise[None, :, None]
    shape = (CLIPS, TOKENS, H * HD)
    drawn = jax.random.normal(key, shape, jnp.float32)
    return jnp.clip(0.3 * drawn * rise, -16.0, 16.0).astype(jnp.bfloat16)


def plant(result, stream_key, least, high):
    longest = result.shape.index(max(result.shape))
    spots = []
    for shift in (0, 1):
        where = [jax.random.randint(jax.random.fold_in(stream_key, axis), (), 0, length) for axis, length in enumerate(result.shape)]
        where[longest] = (where[longest] + shift) % result.shape[longest]
        spots.append(tuple(where))
    return result.at[spots[0]].set(least).at[spots[1]].set(high)


def steps_of(rng, shape, cuts, low, top_value):
    level, own = 1.0, jax.random.fold_in(rng, 6)
    for dim, parts in cuts:
        heights = jnp.exp(jax.random.uniform(jax.random.fold_in(own, dim), (parts,), jnp.float32, low / len(cuts), top_value / len(cuts)))
        level = level * jnp.repeat(heights, shape[dim] // parts).reshape([-1 if axis == dim else 1 for axis in range(len(shape))])
    return level


def scatter_about(stream_key, dims, scale, reach, pieces=(), held_as=jnp.bfloat16):
    result = jax.random.normal(stream_key, dims, jnp.float32) * scale
    if len(pieces) > 0:
        result = steps_of(stream_key, dims, pieces, -0.22, 0.18) * result
    return jnp.clip(result, min=-reach, max=reach).astype(held_as)


def setup_inputs(seed: int = 0) -> dict:
    key_of = jax.random.split(jax.random.key(seed), 9)
    return {
        "queries": draw_queries(jax.random.fold_in(key_of[8], 71), 0),
        "key_rows": draw_key_rows(jax.random.fold_in(key_of[8], 71), 0),
        "value_rows": scatter_about(key_of[2], (CLIPS, TOKENS, HH), 1.0, 6.0, ((0, 16), (1, 16))),
        "grad_out": draw_grad_out(jax.random.fold_in(key_of[8], 71), 0),
        "query_gain": draw_query_gain(jax.random.fold_in(key_of[8], 71), 0),
        "key_gain": draw_key_gain(jax.random.fold_in(key_of[8], 71), 0),
        "valid_frames": plant(jax.random.randint(key_of[6], (CLIPS, SLABS), 1, TT * TF + 1), jax.random.fold_in(key_of[6], 1), 1, TT * TF).astype(jnp.int32),
        "window_start": plant(jax.random.randint(key_of[7], (CLIPS, SLABS * TILES_SLAB), 0, GW - WW + 1), jax.random.fold_in(key_of[7], 1), 0, GW - WW).astype(jnp.int32),
    }


EPSILON = 1e-06

def rounded(array):
    return lax.optimization_barrier(array.astype(jnp.bfloat16)).astype(jnp.float32)

def normalize(rows, gain):
    tokens = rows.shape[0]
    values = rows.astype(jnp.float32).reshape(tokens, H, HD)
    scale = lax.rsqrt(lax.optimization_barrier(jnp.mean(values * values, axis=-1, keepdims=True)) + EPSILON)
    return (values, scale, rounded(values * scale * gain))

def norm_back(values, scale, gain, upstream):
    weighted = gain * upstream
    inner = lax.optimization_barrier(jnp.mean(values * weighted, axis=-1, keepdims=True))
    grad = scale * weighted - values * scale * scale * scale * inner
    return (grad, lax.optimization_barrier(jnp.sum(upstream * values * scale, axis=(0, 1))))

def live_keys(nearby):
    frame_in = (jnp.arange(TILE) // (TH * TW)).astype(jnp.int32)
    first = jnp.concatenate([jnp.full((1,), TT - 1, jnp.int32), jnp.arange(TT).astype(jnp.int32), jnp.zeros((1,), jnp.int32)]) * TF
    counts = jnp.concatenate([nearby[0:1], jnp.repeat(nearby[1:2], TT), nearby[2:3]]).astype(jnp.int32)
    return first[:, None] + frame_in[None, :] < counts[:, None]

def choose_columns(starts):
    offsets = starts.astype(jnp.float32)[:, None, None] + jnp.arange(WW).astype(jnp.float32)[None, :, None]
    return (offsets == jnp.arange(GW).astype(jnp.float32)[None, None, :]).astype(jnp.float32)

def window_rows(tiles, select):
    picked = jnp.einsum('qjw,eawtx->qeajtx', select, tiles)
    return picked.reshape(select.shape[0], -1, H, HD)

def window_mask(valid):
    return jnp.broadcast_to(valid[:, None, None, :], (valid.shape[0], GH, WW, TILE)).reshape(-1)

def scatter_window(terms, select):
    count = terms.shape[0]
    shaped = terms.reshape(count, -1, GH, WW, TILE, H * HD)
    spread = jnp.einsum('qjw,qeajtx->eawtx', select, shaped)
    return spread.reshape(-1, H, HD)

def group_pass(queries, grads, key_tiles, value_tiles, valid, starts):
    root = 1.0 / math.sqrt(HD)
    select = choose_columns(starts)
    window_keys = window_rows(key_tiles, select)
    window_values = window_rows(value_tiles, select)
    mask = window_mask(valid)
    scores = jnp.einsum('qthd,qkhd->qhtk', queries, window_keys) * root
    peak = lax.optimization_barrier(jnp.max(jnp.where(mask, scores, -jnp.inf), axis=-1, keepdims=True))
    weights = jnp.where(mask, jnp.exp(scores - peak), 0.0)
    total = lax.optimization_barrier(jnp.sum(weights, axis=-1, keepdims=True))
    probs = weights / total
    probs_low = rounded(probs)
    attended = jnp.einsum('qhtk,qkhd->qthd', probs_low, window_values)
    slope = jnp.einsum('qthd,qkhd->qhtk', grads, window_values)
    delta = lax.optimization_barrier(jnp.sum(probs * slope, axis=-1, keepdims=True))
    change = rounded(probs * (slope - delta))
    grad_queries = jnp.einsum('qhtk,qkhd->qthd', change, window_keys) * root
    key_window = jnp.einsum('qhtk,qthd->qkhd', change, queries) * root
    value_window = jnp.einsum('qhtk,qthd->qkhd', probs_low, grads)
    return (attended, grad_queries, scatter_window(key_window, select), scatter_window(value_window, select))

def slab_pass(inputs):
    query_norm, grads, key_ext, value_ext, nearby, starts = inputs
    span = GH * GW * TILE
    valid = live_keys(nearby)
    key_tiles = key_ext.reshape(TT + 2, GH, GW, TILE, H * HD)
    value_tiles = value_ext.reshape(TT + 2, GH, GW, TILE, H * HD)
    query_tiles = query_norm.reshape(TT, GH * GW, TILE, H, HD)
    grad_tiles = grads.reshape(TT, GH * GW, TILE, H, HD)
    start_tiles = starts.reshape(TT, GH * GW)
    outputs = []
    query_grads = []
    grad_key_ext = jnp.zeros(((TT + 2) * span, H, HD), jnp.float32)
    grad_value_ext = jnp.zeros(((TT + 2) * span, H, HD), jnp.float32)
    for index in range(TT):
        attended, grad_part, key_part, value_part = group_pass(query_tiles[index], grad_tiles[index], key_tiles[index:index + 3], value_tiles[index:index + 3], valid[index:index + 3], start_tiles[index])
        margins = ((index * span, (TT - 1 - index) * span), (0, 0), (0, 0))
        grad_key_ext = grad_key_ext + jnp.pad(key_part, margins)
        grad_value_ext = grad_value_ext + jnp.pad(value_part, margins)
        outputs.append(attended)
        query_grads.append(grad_part)
    return (jnp.stack(outputs).reshape(SLAB_TOK, H * HD), jnp.stack(query_grads).reshape(SLAB_TOK, H, HD), grad_key_ext, grad_value_ext)

def extend(slabs, span):
    blank = jnp.zeros((1, span, H * HD), jnp.float32)
    before = jnp.concatenate([blank, slabs[:-1, SLAB_TOK - span:]], axis=0)
    after = jnp.concatenate([slabs[1:, :span], blank], axis=0)
    return jnp.concatenate([before, slabs, after], axis=1)

def collect_own(ext, span):
    own = ext[:, span:span + SLAB_TOK]
    blank = jnp.zeros((1, span, H, HD), jnp.float32)
    from_before = jnp.concatenate([blank, ext[:-1, span + SLAB_TOK:]], axis=0)
    from_after = jnp.concatenate([ext[1:, :span], blank], axis=0)
    own = own.at[:, :span].add(from_before)
    own = own.at[:, SLAB_TOK - span:].add(from_after)
    return own.reshape(TOKENS, H, HD)

def reference(queries, key_rows, value_rows, grad_out, query_gain, key_gain, valid_frames, window_start):
    span = GH * GW * TILE

    def one_clip(inputs):
        query_clip, key_clip, value_clip, grad_clip, counts, starts = inputs
        query_values, query_scale, query_norm = normalize(query_clip, query_gain)
        key_values, key_scale, key_norm = normalize(key_clip, key_gain)
        padded = jnp.pad(counts.astype(jnp.int32), 1)
        nearby = jnp.stack([padded[:-2], padded[1:-1], padded[2:]], axis=1)
        key_ext = extend(key_norm.reshape(SLABS, SLAB_TOK, H * HD), span)
        value_ext = extend(value_clip.astype(jnp.float32).reshape(SLABS, SLAB_TOK, H * HD), span)
        results = lax.map(slab_pass, (query_norm.reshape(SLABS, SLAB_TOK, H, HD), grad_clip.astype(jnp.float32).reshape(SLABS, SLAB_TOK, H, HD), key_ext, value_ext, nearby, starts.reshape(SLABS, TILES_SLAB)))
        attended, query_grads, grad_key_ext, grad_value_ext = results
        grad_query, query_part = norm_back(query_values, query_scale, query_gain, query_grads.reshape(TOKENS, H, HD))
        grad_key, key_part = norm_back(key_values, key_scale, key_gain, collect_own(grad_key_ext, span))
        grad_value = collect_own(grad_value_ext, span)
        return (attended.reshape(TOKENS, H * HD).astype(jnp.bfloat16), grad_query.reshape(TOKENS, H * HD).astype(jnp.bfloat16), grad_key.reshape(TOKENS, H * HD).astype(jnp.bfloat16), grad_value.reshape(TOKENS, H * HD).astype(jnp.bfloat16), query_part, key_part)
    results = lax.map(one_clip, (queries, key_rows, value_rows, grad_out, valid_frames, window_start))
    return (results[0], results[1], results[2], results[3], lax.optimization_barrier(jnp.sum(results[4], axis=0)), lax.optimization_barrier(jnp.sum(results[5], axis=0)))
```

```python
import functools
import math

import jax
import jax.numpy as jnp
from jax import lax
from jax.experimental import pallas as pl
from jax.experimental.pallas import tpu as pltpu
from jax.sharding import PartitionSpec as P

MESH = pl.DeviceIdType.MESH
H = 12
HD = 128
GW = 4
WW = 2
TILE = 64
FRAME = 16
TOK = 256
HH = 1536
N_TM = 16
N_CLIP = 16
EPSILON = 1e-06
ROOT = 1.0 / math.sqrt(HD)
SCALE = ROOT * math.log2(math.e)
DEAD = -1e30
GROUPS = 3
PER = H // GROUPS
GCOLS = PER * HD

NT = (((1,), (1,)), ((), ()))
TN = (((0,), (0,)), ((), ()))


def dot(a, b, dims=(((1,), (0,)), ((), ()))):
    return lax.dot_general(a, b, dims, preferred_element_type=jnp.float32)


def cols(h):
    return pl.ds(pl.multiple_of(h * HD, HD), HD)


def group_cols(g):
    return pl.ds(pl.multiple_of(g * GCOLS, GCOLS), GCOLS)


def inv_rms(values):
    return lax.rsqrt(jnp.mean(values * values, axis=-1, keepdims=True) + EPSILON)


def norm_back(values, scale, gain, upstream):
    weighted = gain * upstream
    inner = jnp.mean(values * weighted, axis=-1, keepdims=True)
    return scale * weighted - values * (scale * scale * scale * inner)


def fold(rows):
    return jnp.sum(rows.reshape(TOK // 8, 8, HD), axis=0)


def main_kernel(
    q_hbm, k_hbm, v_hbm, g_hbm, q_gain, k_gain, frames, starts,
    att_out, dq_out, dk_out, dv_out, gains_out,
    raw, halo, qn_own, kn_own, acc, stage, bias_f, bias_b,
    stat_cols, stat_mine, stat_halo, gain_acc, part, ring_in, clip_in, total,
    load_sem, out_sem, send_sem, recv_sem, stat_send, stat_recv,
    ready, ring_send, ring_recv, clip_send, clip_recv, total_send, total_recv,
):
    me = lax.axis_index("tm")
    clip = lax.axis_index("clip")
    has_left = me > 0
    has_right = me < N_TM - 1
    loads = []
    for i, ref in enumerate((q_hbm, k_hbm, v_hbm, g_hbm)):
        load = pltpu.make_async_copy(ref.at[0], raw.at[i], load_sem.at[i])
        load.start()
        loads.append(load)

    barrier = pltpu.get_barrier_semaphore()

    @pl.when(has_left)
    def _():
        pl.semaphore_signal(barrier, inc=1, device_id={"tm": me - 1}, device_id_type=MESH)

    @pl.when(has_right)
    def _():
        pl.semaphore_signal(barrier, inc=1, device_id={"tm": me + 1}, device_id_type=MESH)

    @pl.when(me > 1)
    def _():
        pl.semaphore_signal(barrier, inc=1, device_id={"tm": 0}, device_id_type=MESH)

    @pl.when(me == 0)
    def _():
        for j in range(1, N_CLIP):
            pl.semaphore_signal(
                barrier, inc=1, device_id={"clip": lax.rem(clip + j, N_CLIP)}, device_id_type=MESH
            )
        pl.semaphore_wait(barrier, N_TM - 1 + N_CLIP - 1)
        for i in range(1, N_TM):
            pl.semaphore_signal(ready, inc=1, device_id={"tm": i}, device_id_type=MESH)

    @pl.when(jnp.logical_and(has_left, has_right))
    def _():
        pl.semaphore_wait(barrier, 2)

    @pl.when(me == N_TM - 1)
    def _():
        pl.semaphore_wait(barrier, 1)

    def transfer(side, a, g):
        source = qn_own if a == 3 else (k_hbm, v_hbm, g_hbm)[a].at[0]
        return pltpu.make_async_remote_copy(
            src_ref=source.at[:, group_cols(g)],
            dst_ref=halo.at[1 - side, a, :, group_cols(g)],
            send_sem=send_sem.at[side, a, g],
            recv_sem=recv_sem.at[1 - side, a, g],
            device_id={"tm": me + (1 if side else -1)},
            device_id_type=MESH,
        )

    def stat_transfer(side, g):
        return pltpu.make_async_remote_copy(
            src_ref=stat_mine.at[g],
            dst_ref=stat_halo.at[1 - side, g],
            send_sem=stat_send.at[side, g],
            recv_sem=stat_recv.at[1 - side, g],
            device_id={"tm": me + (1 if side else -1)},
            device_id_type=MESH,
        )

    def send(arrays, g):
        for side, present in ((0, has_left), (1, has_right)):

            @pl.when(present)
            def _():
                for a in arrays:
                    transfer(side, a, g).start()

    def receive(arrays, g):
        for side, present in ((0, has_left), (1, has_right)):

            @pl.when(present)
            def _():
                for a in arrays:
                    transfer(1 - side, a, g).wait_recv()

    for g in range(GROUPS):
        send((0, 1), g)

    for side, present in ((0, has_left), (1, has_right)):

        @pl.when(jnp.logical_not(present))
        def _():
            halo[side] = jnp.zeros((4, TOK, HH), jnp.bfloat16)
            stat_halo[side] = jnp.zeros((GROUPS, 8, TOK), jnp.float32)

    rows = lax.broadcasted_iota(jnp.int32, (TOK, TOK), 0)
    lanes = lax.broadcasted_iota(jnp.int32, (TOK, TOK), 1)

    def window_of(where, position, present):
        chosen = jnp.zeros((TOK, TOK), jnp.int32)
        for t in range(GW):
            start = starts[0, position * GW + t]
            chosen = jnp.where(where // TILE == t, jnp.where(present, start, -100), chosen)
        return chosen

    def bias_of(window, keys, count):
        column = keys // TILE
        frame = (keys % TILE) // FRAME
        live = (column >= window) & (column < window + WW) & (frame < count)
        return jnp.where(live, 0.0, DEAD).astype(jnp.float32)

    before = jnp.maximum(me - 1, 0)
    after = jnp.minimum(me + 1, N_TM - 1)
    mine = window_of(rows, me, me >= 0)
    count_own = frames[0, me]
    bias_f[0] = bias_of(mine, lanes, jnp.where(has_left, frames[0, before], 0))
    bias_f[1] = bias_of(mine, lanes, count_own)
    bias_f[2] = bias_of(mine, lanes, jnp.where(has_right, frames[0, after], 0))
    bias_b[0] = bias_of(window_of(lanes, before, has_left), rows, count_own)
    bias_b[1] = bias_of(window_of(lanes, after, has_right), rows, count_own)

    gain_acc[...] = jnp.zeros_like(gain_acc)
    stat_cols[...] = jnp.zeros_like(stat_cols)
    gain_q = q_gain[...]
    gain_k = k_gain[...]
    ungain_k = 1.0 / gain_k
    for load in loads:
        load.wait()

    def normal_queries(h, carry):
        values = raw[0, :, cols(h)].astype(jnp.float32)
        qn_own[:, cols(h)] = (values * inv_rms(values) * gain_q).astype(jnp.bfloat16)
        return carry

    lax.fori_loop(0, H, normal_queries, 0)

    stat_lane = lax.broadcasted_iota(jnp.int32, (TOK, HD), 1)

    def forward_head(local, g):
        h = g * PER + local
        at = cols(h)
        qn = qn_own[:, at]
        grads = raw[3, :, at]
        keys, extras, values = [], [], []
        for p in range(3):
            rough = (halo[0, 0, :, at], raw[1, :, at], halo[1, 0, :, at])[p].astype(jnp.float32)
            hat = rough * inv_rms(rough)
            kn = (hat * gain_k).astype(jnp.bfloat16)
            keys.append(kn)
            extras.append((hat - kn.astype(jnp.float32) * ungain_k).astype(jnp.bfloat16))
            values.append((halo[0, 1, :, at], raw[2, :, at], halo[1, 1, :, at])[p])
        kn_own[:, at] = keys[1]
        scores = [dot(qn, keys[p], NT) * SCALE + bias_f[p] for p in range(3)]
        peak = jnp.max(jnp.maximum(jnp.maximum(scores[0], scores[1]), scores[2]), axis=-1, keepdims=True)
        weights = [jnp.exp2(s - peak) for s in scores]
        mass = jnp.sum(weights[0] + weights[1] + weights[2], axis=-1, keepdims=True)
        inverse = 1.0 / mass
        probs = [w * inverse for w in weights]
        slopes = [dot(grads, values[p], NT) for p in range(3)]
        delta = jnp.sum(
            probs[0] * slopes[0] + probs[1] * slopes[1] + probs[2] * slopes[2], axis=-1, keepdims=True
        )
        low = [x.astype(jnp.bfloat16) for x in probs]
        change = [(probs[p] * (slopes[p] - delta)).astype(jnp.bfloat16) for p in range(3)]
        stage[0, :, at] = sum(dot(low[p], values[p]) for p in range(3)).astype(jnp.bfloat16)
        wide = sum(
            dot(change[p], jnp.concatenate([keys[p], extras[p]], axis=1)) for p in range(3)
        )
        dqn = wide[:, :HD] * ROOT
        by_hat = dqn * ungain_k + wide[:, HD:] * ROOT
        query = raw[0, :, at].astype(jnp.float32)
        scale = inv_rms(query)
        gain_acc[0] += fold(dqn * query * scale)
        gain_acc[1] += fold(qn.astype(jnp.float32) * by_hat)
        stage[1, :, at] = norm_back(query, scale, gain_q, dqn).astype(jnp.bfloat16)
        acc[0, :, at] = dot(change[1], qn, TN)
        acc[1, :, at] = dot(low[1], grads, TN)
        logs = peak + jnp.log2(mass)
        kept = stat_cols[...]
        kept = jnp.where(stat_lane == 2 * local, logs, kept)
        stat_cols[...] = jnp.where(stat_lane == 2 * local + 1, delta, kept)
        return g

    def out_copy(ref, i, g):
        return pltpu.make_async_copy(
            stage.at[i, :, group_cols(g)], ref.at[0, :, group_cols(g)], out_sem.at[i, g]
        )

    def forward_group(g, carry):
        receive((0, 1), g)
        send((2, 3), g)
        lax.fori_loop(0, PER, forward_head, g)
        stat_mine[g] = jnp.transpose(stat_cols[...])[:8]
        for side, present in ((0, has_left), (1, has_right)):

            @pl.when(present)
            def _():
                stat_transfer(side, g).start()

        out_copy(att_out, 0, g).start()
        out_copy(dq_out, 1, g).start()
        return carry

    lax.fori_loop(0, GROUPS, forward_group, 0)

    row8 = lax.broadcasted_iota(jnp.int32, (8, HD), 0)
    query_part = jnp.sum(gain_acc[0], axis=0, keepdims=True)
    key_part = jnp.sum(gain_acc[1], axis=0, keepdims=True)
    part[...] = jnp.where(row8 == 0, query_part, jnp.where(row8 == 1, key_part, 0.0))

    def to_ring(i):
        return pltpu.make_async_remote_copy(
            src_ref=part, dst_ref=ring_in.at[i], send_sem=ring_send, recv_sem=ring_recv.at[i],
            device_id={"tm": 0}, device_id_type=MESH,
        )

    @pl.when(has_left)
    def _():
        pl.semaphore_wait(ready, 1)
        to_ring(me).start()

    def backward_head(local, g):
        h = g * PER + local
        at = cols(h)
        kn = kn_own[:, at]
        values = raw[2, :, at]
        dk = acc[0, :, at]
        dv = acc[1, :, at]
        for side in range(2):
            qn = halo[side, 3, :, at]
            grads = halo[side, 2, :, at]
            logs = stat_halo[side, g, pl.ds(2 * local, 1), :]
            delta = stat_halo[side, g, pl.ds(2 * local + 1, 1), :]
            probs = jnp.exp2(dot(kn, qn, NT) * SCALE + bias_b[side] - logs)
            slopes = dot(values, grads, NT)
            change = (probs * (slopes - delta)).astype(jnp.bfloat16)
            dk = dk + dot(change, qn)
            dv = dv + dot(probs.astype(jnp.bfloat16), grads)
        rough = raw[1, :, at].astype(jnp.float32)
        stage[2, :, at] = norm_back(rough, inv_rms(rough), gain_k, dk * ROOT).astype(jnp.bfloat16)
        stage[3, :, at] = dv.astype(jnp.bfloat16)
        return g

    def backward_group(g, carry):
        for side, present in ((0, has_left), (1, has_right)):

            @pl.when(present)
            def _():
                stat_transfer(1 - side, g).wait_recv()

        receive((2, 3), g)
        lax.fori_loop(0, PER, backward_head, g)
        out_copy(dk_out, 2, g).start()
        out_copy(dv_out, 3, g).start()
        return carry

    lax.fori_loop(0, GROUPS, backward_group, 0)

    def to_clip(j, slot):
        return pltpu.make_async_remote_copy(
            src_ref=clip_in.at[clip], dst_ref=clip_in.at[slot], send_sem=clip_send.at[j],
            recv_sem=clip_recv.at[slot], device_id={"clip": lax.rem(clip + j, N_CLIP)},
            device_id_type=MESH,
        )

    def to_all(i):
        return pltpu.make_async_remote_copy(
            src_ref=total, dst_ref=total, send_sem=total_send.at[i], recv_sem=total_recv,
            device_id={"tm": i}, device_id_type=MESH,
        )

    @pl.when(me == 0)
    def _():
        ring = part[...]
        for i in range(1, N_TM):
            to_ring(i).wait_recv()
            ring = ring + ring_in[i]
        clip_in[clip] = ring
        for j in range(1, N_CLIP):
            to_clip(j, clip).start()
        for j in range(1, N_CLIP):
            to_clip(j, lax.rem(clip + j, N_CLIP)).wait_recv()
        everything = clip_in[0]
        for c in range(1, N_CLIP):
            everything = everything + clip_in[c]
        total[...] = everything
        for i in range(1, N_TM):
            to_all(i).start()
        for j in range(1, N_CLIP):
            to_clip(j, clip).wait_send()
        for i in range(1, N_TM):
            to_all(i).wait_send()

    @pl.when(has_left)
    def _():
        to_all(0).wait_recv()
        to_ring(me).wait_send()

    gains_out[...] = total[...]
    for side, present in ((0, has_left), (1, has_right)):

        @pl.when(present)
        def _():
            for g in range(GROUPS):
                for a in range(4):
                    transfer(side, a, g).wait_send()
                stat_transfer(side, g).wait_send()

    for i, ref in enumerate((att_out, dq_out, dk_out, dv_out)):
        for g in range(GROUPS):
            out_copy(ref, i, g).wait()


def finish_kernel(*refs):
    ins, gains, outs, q_total, k_total = refs[:4], refs[4], refs[5:9], refs[9], refs[10]
    held, in_sem, out_sem = refs[11:]
    reads = [pltpu.make_async_copy(ins[i], held.at[i], in_sem.at[i]) for i in range(4)]
    writes = [pltpu.make_async_copy(held.at[i], outs[i], out_sem.at[i]) for i in range(4)]
    for read in reads:
        read.start()
    q_total[...] = gains[0:1]
    k_total[...] = gains[1:2]
    for read, write in zip(reads, writes):
        read.wait()
        write.start()
    for write in writes:
        write.wait()


def on_device(
    queries, key_rows, value_rows, grad_out, query_gain, key_gain, valid_frames, window_start
):
    any_spec = pl.BlockSpec(memory_space=pl.ANY)
    vmem_spec = pl.BlockSpec(memory_space=pltpu.VMEM)
    smem_spec = pl.BlockSpec(memory_space=pltpu.SMEM)
    slab = jax.ShapeDtypeStruct((1, TOK, HH), jnp.bfloat16)
    dma = pltpu.SemaphoreType.DMA
    bf16, f32 = jnp.bfloat16, jnp.float32
    results = pl.pallas_call(
        main_kernel,
        out_shape=[slab] * 4 + [jax.ShapeDtypeStruct((8, HD), f32)],
        in_specs=[any_spec] * 4 + [vmem_spec] * 2 + [smem_spec] * 2,
        out_specs=[any_spec] * 4 + [vmem_spec],
        scratch_shapes=[
            pltpu.VMEM((4, TOK, HH), bf16),
            pltpu.VMEM((2, 4, TOK, HH), bf16),
            pltpu.VMEM((TOK, HH), bf16),
            pltpu.VMEM((TOK, HH), bf16),
            pltpu.VMEM((2, TOK, HH), f32),
            pltpu.VMEM((4, TOK, HH), bf16),
            pltpu.VMEM((3, TOK, TOK), f32),
            pltpu.VMEM((2, TOK, TOK), f32),
            pltpu.VMEM((TOK, HD), f32),
            pltpu.VMEM((GROUPS, 8, TOK), f32),
            pltpu.VMEM((2, GROUPS, 8, TOK), f32),
            pltpu.VMEM((2, 8, HD), f32),
            pltpu.VMEM((8, HD), f32),
            pltpu.VMEM((N_TM, 8, HD), f32),
            pltpu.VMEM((N_CLIP, 8, HD), f32),
            pltpu.VMEM((8, HD), f32),
            dma((4,)),
            dma((4, GROUPS)),
            dma((2, 4, GROUPS)),
            dma((2, 4, GROUPS)),
            dma((2, GROUPS)),
            dma((2, GROUPS)),
            pltpu.SemaphoreType.REGULAR,
            dma,
            dma((N_TM,)),
            dma((N_CLIP,)),
            dma((N_CLIP,)),
            dma((N_TM,)),
            dma,
        ],
        compiler_params=pltpu.CompilerParams(
            collective_id=0, has_side_effects=True, vmem_limit_bytes=58 * 2**20
        ),
        name="attend",
    )(
        queries, key_rows, value_rows, grad_out,
        query_gain.reshape(1, HD), key_gain.reshape(1, HD), valid_frames, window_start,
    )
    row = jax.ShapeDtypeStruct((1, HD), f32)
    outs = pl.pallas_call(
        finish_kernel,
        out_shape=[slab] * 4 + [row] * 2,
        in_specs=[any_spec] * 4 + [vmem_spec],
        out_specs=[any_spec] * 4 + [vmem_spec] * 2,
        scratch_shapes=[pltpu.VMEM((4, 1, TOK, HH), bf16), dma((4,)), dma((4,))],
        compiler_params=pltpu.CompilerParams(vmem_limit_bytes=56 * 2**20),
        name="finish",
    )(*results)
    return (*outs[:4], outs[4].reshape(HD), outs[5].reshape(HD))


def solution(mesh):
    slabs = P("clip", "tm", None)
    return jax.shard_map(
        on_device,
        mesh=mesh,
        in_specs=(slabs,) * 4 + (P(), P(), P("clip", None), P("clip", None)),
        out_specs=(slabs,) * 4 + (P(), P()),
        check_vma=False,
    )
```

```python
import functools
import math

import jax
import jax.numpy as jnp
from jax import lax
from jax.experimental import pallas as pl
from jax.experimental.pallas import tpu as pltpu
from jax.sharding import PartitionSpec as P

MESH = pl.DeviceIdType.MESH
H = 12
HD = 128
GW = 4
WW = 2
TILE = 64
FRAME = 16
TOK = 256
HH = 1536
N_TM = 16
N_CLIP = 16
EPSILON = 1e-06
ROOT = 1.0 / math.sqrt(HD)
SCALE = ROOT * math.log2(math.e)
DEAD = -1e30
GROUPS = 6
AHEAD = 2
PER = H // GROUPS
GCOLS = PER * HD

NT = (((1,), (1,)), ((), ()))
TN = (((0,), (0,)), ((), ()))


def dot(a, b, dims=(((1,), (0,)), ((), ()))):
    return lax.dot_general(a, b, dims, preferred_element_type=jnp.float32)


def cols(h):
    return pl.ds(pl.multiple_of(h * HD, HD), HD)


def group_cols(g):
    return pl.ds(pl.multiple_of(g * GCOLS, GCOLS), GCOLS)


def inv_rms(values):
    return lax.rsqrt(jnp.mean(values * values, axis=-1, keepdims=True) + EPSILON)


def norm_back(values, scale, gain, upstream):
    weighted = gain * upstream
    inner = jnp.mean(values * weighted, axis=-1, keepdims=True)
    return scale * weighted - values * (scale * scale * scale * inner)


def fold(rows):
    return jnp.sum(rows.reshape(TOK // 8, 8, HD), axis=0)


def main_kernel(
    q_hbm, k_hbm, v_hbm, g_hbm, q_gain, k_gain, frames, starts,
    att_out, dq_out, dk_out, dv_out, gains_out,
    raw, halo, qn_own, kn_own, acc, stage, bias_f, bias_b,
    stat_cols, stat_mine, stat_halo, gain_acc, part, ring_in, clip_in, total,
    load_sem, out_sem, send_sem, recv_sem, stat_send, stat_recv,
    ready, ring_send, ring_recv, clip_send, clip_recv, total_send, total_recv,
):
    me = lax.axis_index("tm")
    clip = lax.axis_index("clip")
    step = 1 - 2 * lax.rem(me, 2)
    near = me + step
    far = me - step
    has_far = jnp.logical_and(me > 0, me < N_TM - 1)
    sides = (near, far)
    loads = []
    for i, ref in enumerate((q_hbm, k_hbm, v_hbm, g_hbm)):
        load = pltpu.make_async_copy(ref.at[0], raw.at[i], load_sem.at[i])
        load.start()
        loads.append(load)

    barrier = pltpu.get_barrier_semaphore()

    pl.semaphore_signal(barrier, inc=1, device_id={"tm": near}, device_id_type=MESH)

    @pl.when(has_far)
    def _():
        pl.semaphore_signal(barrier, inc=1, device_id={"tm": far}, device_id_type=MESH)

    @pl.when(me > 1)
    def _():
        pl.semaphore_signal(barrier, inc=1, device_id={"tm": 0}, device_id_type=MESH)

    @pl.when(me == 0)
    def _():
        for j in range(1, N_CLIP):
            pl.semaphore_signal(
                barrier, inc=1, device_id={"clip": lax.rem(clip + j, N_CLIP)}, device_id_type=MESH
            )
        pl.semaphore_wait(barrier, N_TM - 1 + N_CLIP - 1)
        for i in range(1, N_TM):
            pl.semaphore_signal(ready, inc=1, device_id={"tm": i}, device_id_type=MESH)

    @pl.when(has_far)
    def _():
        pl.semaphore_wait(barrier, 2)

    @pl.when(me == N_TM - 1)
    def _():
        pl.semaphore_wait(barrier, 1)

    def transfer(side, a, g):
        source = qn_own if a == 3 else (k_hbm, v_hbm, g_hbm)[a].at[0]
        return pltpu.make_async_remote_copy(
            src_ref=source.at[:, group_cols(g)],
            dst_ref=halo.at[side, a, :, group_cols(g)],
            send_sem=send_sem.at[side, a, g],
            recv_sem=recv_sem.at[side, a, g],
            device_id={"tm": sides[side]},
            device_id_type=MESH,
        )

    def stat_transfer(side, g):
        return pltpu.make_async_remote_copy(
            src_ref=stat_mine.at[g],
            dst_ref=stat_halo.at[side, g],
            send_sem=stat_send.at[side, g],
            recv_sem=stat_recv.at[side, g],
            device_id={"tm": sides[side]},
            device_id_type=MESH,
        )

    def send_near(a):
        for g in range(GROUPS):
            transfer(0, a, g).start()

    def send_far(arrays, g):
        @pl.when(has_far)
        def _():
            for a in arrays:
                transfer(1, a, g).start()

    def receive(arrays, g):
        for a in arrays:
            transfer(0, a, g).wait_recv()

        @pl.when(has_far)
        def _():
            for a in arrays:
                transfer(1, a, g).wait_recv()

    for g in range(AHEAD):
        send_far((0, 1), g)
    for a in (0, 1, 2):
        send_near(a)

    @pl.when(jnp.logical_not(has_far))
    def _():
        halo[1] = jnp.zeros((4, TOK, HH), jnp.bfloat16)
        stat_halo[1] = jnp.zeros((GROUPS, 8, TOK), jnp.float32)

    rows = lax.broadcasted_iota(jnp.int32, (TOK, TOK), 0)
    lanes = lax.broadcasted_iota(jnp.int32, (TOK, TOK), 1)

    def window_of(where, position, present):
        chosen = jnp.zeros((TOK, TOK), jnp.int32)
        for t in range(GW):
            start = starts[0, position * GW + t]
            chosen = jnp.where(where // TILE == t, jnp.where(present, start, -100), chosen)
        return chosen

    def bias_of(window, keys, count):
        column = keys // TILE
        frame = (keys % TILE) // FRAME
        live = (column >= window) & (column < window + WW) & (frame < count)
        return jnp.where(live, 0.0, DEAD).astype(jnp.float32)

    known = jnp.where(has_far, far, me)
    mine = window_of(rows, me, me >= 0)
    count_own = frames[0, me]
    bias_f[0] = bias_of(mine, lanes, frames[0, near])
    bias_f[1] = bias_of(mine, lanes, count_own)
    bias_f[2] = bias_of(mine, lanes, jnp.where(has_far, frames[0, known], 0))
    bias_b[0] = bias_of(window_of(lanes, near, me >= 0), rows, count_own)
    bias_b[1] = bias_of(window_of(lanes, known, has_far), rows, count_own)

    gain_acc[...] = jnp.zeros_like(gain_acc)
    stat_cols[...] = jnp.zeros_like(stat_cols)
    gain_q = q_gain[...]
    gain_k = k_gain[...]
    ungain_k = 1.0 / gain_k
    for load in loads:
        load.wait()

    def normal_queries(h, carry):
        values = raw[0, :, cols(h)].astype(jnp.float32)
        qn_own[:, cols(h)] = (values * inv_rms(values) * gain_q).astype(jnp.bfloat16)
        return carry

    lax.fori_loop(0, H, normal_queries, 0)
    send_near(3)

    stat_lane = lax.broadcasted_iota(jnp.int32, (TOK, HD), 1)

    def forward_head(local, g):
        h = g * PER + local
        at = cols(h)
        qn = qn_own[:, at]
        grads = raw[3, :, at]
        keys, extras, values = [], [], []
        for p in range(3):
            rough = (halo[0, 0, :, at], raw[1, :, at], halo[1, 0, :, at])[p].astype(jnp.float32)
            hat = rough * inv_rms(rough)
            kn = (hat * gain_k).astype(jnp.bfloat16)
            keys.append(kn)
            extras.append((hat - kn.astype(jnp.float32) * ungain_k).astype(jnp.bfloat16))
            values.append((halo[0, 1, :, at], raw[2, :, at], halo[1, 1, :, at])[p])
        kn_own[:, at] = keys[1]
        scores = [dot(qn, keys[p], NT) * SCALE + bias_f[p] for p in range(3)]
        peak = jnp.max(jnp.maximum(jnp.maximum(scores[0], scores[1]), scores[2]), axis=-1, keepdims=True)
        weights = [jnp.exp2(s - peak) for s in scores]
        mass = jnp.sum(weights[0] + weights[1] + weights[2], axis=-1, keepdims=True)
        inverse = 1.0 / mass
        probs = [w * inverse for w in weights]
        slopes = [dot(grads, values[p], NT) for p in range(3)]
        delta = jnp.sum(
            probs[0] * slopes[0] + probs[1] * slopes[1] + probs[2] * slopes[2], axis=-1, keepdims=True
        )
        low = [x.astype(jnp.bfloat16) for x in probs]
        change = [(probs[p] * (slopes[p] - delta)).astype(jnp.bfloat16) for p in range(3)]
        stage[0, :, at] = sum(dot(low[p], values[p]) for p in range(3)).astype(jnp.bfloat16)
        wide = sum(
            dot(change[p], jnp.concatenate([keys[p], extras[p]], axis=1)) for p in range(3)
        )
        dqn = wide[:, :HD] * ROOT
        by_hat = dqn * ungain_k + wide[:, HD:] * ROOT
        query = raw[0, :, at].astype(jnp.float32)
        scale = inv_rms(query)
        gain_acc[0] += fold(dqn * query * scale)
        gain_acc[1] += fold(qn.astype(jnp.float32) * by_hat)
        stage[1, :, at] = norm_back(query, scale, gain_q, dqn).astype(jnp.bfloat16)
        acc[0, :, at] = dot(change[1], qn, TN)
        acc[1, :, at] = dot(low[1], grads, TN)
        logs = peak + jnp.log2(mass)
        kept = stat_cols[...]
        kept = jnp.where(stat_lane == 2 * local, logs, kept)
        stat_cols[...] = jnp.where(stat_lane == 2 * local + 1, delta, kept)
        return g

    def out_copy(ref, i, g):
        return pltpu.make_async_copy(
            stage.at[i, :, group_cols(g)], ref.at[0, :, group_cols(g)], out_sem.at[i, g]
        )

    def forward_group(g, carry):
        receive((0, 1), g)

        @pl.when(g + AHEAD < GROUPS)
        def _():
            send_far((0, 1), g + AHEAD)

        @pl.when(g + AHEAD >= GROUPS)
        def _():
            send_far((2, 3), g + AHEAD - GROUPS)

        lax.fori_loop(0, PER, forward_head, g, unroll=True)
        stat_mine[g] = jnp.transpose(stat_cols[...])[:8]
        stat_transfer(0, g).start()

        @pl.when(has_far)
        def _():
            stat_transfer(1, g).start()

        out_copy(att_out, 0, g).start()
        out_copy(dq_out, 1, g).start()
        return carry

    lax.fori_loop(0, GROUPS, forward_group, 0)

    row8 = lax.broadcasted_iota(jnp.int32, (8, HD), 0)
    query_part = jnp.sum(gain_acc[0], axis=0, keepdims=True)
    key_part = jnp.sum(gain_acc[1], axis=0, keepdims=True)
    part[...] = jnp.where(row8 == 0, query_part, jnp.where(row8 == 1, key_part, 0.0))

    def to_ring(i):
        return pltpu.make_async_remote_copy(
            src_ref=part, dst_ref=ring_in.at[i], send_sem=ring_send, recv_sem=ring_recv.at[i],
            device_id={"tm": 0}, device_id_type=MESH,
        )

    @pl.when(me > 0)
    def _():
        pl.semaphore_wait(ready, 1)
        to_ring(me).start()

    def to_clip(j, slot):
        return pltpu.make_async_remote_copy(
            src_ref=clip_in.at[clip], dst_ref=clip_in.at[slot], send_sem=clip_send.at[j],
            recv_sem=clip_recv.at[slot], device_id={"clip": lax.rem(clip + j, N_CLIP)},
            device_id_type=MESH,
        )

    def to_all(i):
        return pltpu.make_async_remote_copy(
            src_ref=total, dst_ref=total, send_sem=total_send.at[i], recv_sem=total_recv,
            device_id={"tm": i}, device_id_type=MESH,
        )

    @pl.when(me == 0)
    def _():
        ring = part[...]
        for i in range(1, N_TM):
            to_ring(i).wait_recv()
            ring = ring + ring_in[i]
        clip_in[clip] = ring
        for j in range(1, N_CLIP):
            to_clip(j, clip).start()

    def share_total():
        for j in range(1, N_CLIP):
            to_clip(j, lax.rem(clip + j, N_CLIP)).wait_recv()
        everything = clip_in[0]
        for c in range(1, N_CLIP):
            everything = everything + clip_in[c]
        total[...] = everything
        for i in range(1, N_TM):
            to_all(i).start()

    def backward_head(local, g):
        h = g * PER + local
        at = cols(h)
        kn = kn_own[:, at]
        values = raw[2, :, at]
        dk = acc[0, :, at]
        dv = acc[1, :, at]
        for side in range(2):
            qn = halo[side, 3, :, at]
            grads = halo[side, 2, :, at]
            logs = stat_halo[side, g, pl.ds(2 * local, 1), :]
            delta = stat_halo[side, g, pl.ds(2 * local + 1, 1), :]
            probs = jnp.exp2(dot(kn, qn, NT) * SCALE + bias_b[side] - logs)
            slopes = dot(values, grads, NT)
            change = (probs * (slopes - delta)).astype(jnp.bfloat16)
            dk = dk + dot(change, qn)
            dv = dv + dot(probs.astype(jnp.bfloat16), grads)
        rough = raw[1, :, at].astype(jnp.float32)
        stage[2, :, at] = norm_back(rough, inv_rms(rough), gain_k, dk * ROOT).astype(jnp.bfloat16)
        stage[3, :, at] = dv.astype(jnp.bfloat16)
        return g

    def backward_group(g, carry):
        stat_transfer(0, g).wait_recv()

        @pl.when(has_far)
        def _():
            stat_transfer(1, g).wait_recv()

        receive((2, 3), g)

        @pl.when(g + AHEAD < GROUPS)
        def _():
            send_far((2, 3), g + AHEAD)

        lax.fori_loop(0, PER, backward_head, g, unroll=True)
        out_copy(dk_out, 2, g).start()
        out_copy(dv_out, 3, g).start()
        return carry

    lax.fori_loop(0, GROUPS, backward_group, 0)

    @pl.when(me == 0)
    def _():
        share_total()


    @pl.when(me > 0)
    def _():
        to_all(0).wait_recv()
        to_ring(me).wait_send()

    @pl.when(me == 0)
    def _():
        for j in range(1, N_CLIP):
            to_clip(j, clip).wait_send()
        for i in range(1, N_TM):
            to_all(i).wait_send()

    gains_out[...] = total[...]
    def all_sent(side):
        for g in range(GROUPS):
            for a in range(4):
                transfer(side, a, g).wait_send()
            stat_transfer(side, g).wait_send()

    all_sent(0)

    @pl.when(has_far)
    def _():
        all_sent(1)

    for i, ref in enumerate((att_out, dq_out, dk_out, dv_out)):
        for g in range(GROUPS):
            out_copy(ref, i, g).wait()


def finish_kernel(*refs):
    ins, gains, outs, q_total, k_total = refs[:4], refs[4], refs[5:9], refs[9], refs[10]
    out_sem = refs[11]
    writes = [pltpu.make_async_copy(ins[i], outs[i], out_sem.at[i]) for i in range(4)]
    for write in writes:
        write.start()
    q_total[...] = gains[0:1]
    k_total[...] = gains[1:2]
    for write in writes:
        write.wait()


def on_device(
    queries, key_rows, value_rows, grad_out, query_gain, key_gain, valid_frames, window_start
):
    any_spec = pl.BlockSpec(memory_space=pl.ANY)
    vmem_spec = pl.BlockSpec(memory_space=pltpu.VMEM)
    smem_spec = pl.BlockSpec(memory_space=pltpu.SMEM)
    slab = jax.ShapeDtypeStruct((1, TOK, HH), jnp.bfloat16)
    dma = pltpu.SemaphoreType.DMA
    bf16, f32 = jnp.bfloat16, jnp.float32
    results = pl.pallas_call(
        main_kernel,
        out_shape=[slab] * 4 + [jax.ShapeDtypeStruct((8, HD), f32)],
        in_specs=[any_spec] * 4 + [vmem_spec] * 2 + [smem_spec] * 2,
        out_specs=[any_spec] * 4 + [vmem_spec],
        scratch_shapes=[
            pltpu.VMEM((4, TOK, HH), bf16),
            pltpu.VMEM((2, 4, TOK, HH), bf16),
            pltpu.VMEM((TOK, HH), bf16),
            pltpu.VMEM((TOK, HH), bf16),
            pltpu.VMEM((2, TOK, HH), f32),
            pltpu.VMEM((4, TOK, HH), bf16),
            pltpu.VMEM((3, TOK, TOK), f32),
            pltpu.VMEM((2, TOK, TOK), f32),
            pltpu.VMEM((TOK, HD), f32),
            pltpu.VMEM((GROUPS, 8, TOK), f32),
            pltpu.VMEM((2, GROUPS, 8, TOK), f32),
            pltpu.VMEM((2, 8, HD), f32),
            pltpu.VMEM((8, HD), f32),
            pltpu.VMEM((N_TM, 8, HD), f32),
            pltpu.VMEM((N_CLIP, 8, HD), f32),
            pltpu.VMEM((8, HD), f32),
            dma((4,)),
            dma((4, GROUPS)),
            dma((2, 4, GROUPS)),
            dma((2, 4, GROUPS)),
            dma((2, GROUPS)),
            dma((2, GROUPS)),
            pltpu.SemaphoreType.REGULAR,
            dma,
            dma((N_TM,)),
            dma((N_CLIP,)),
            dma((N_CLIP,)),
            dma((N_TM,)),
            dma,
        ],
        compiler_params=pltpu.CompilerParams(
            collective_id=0, has_side_effects=True, vmem_limit_bytes=203 * 2**18
        ),
        name="attend",
    )(
        queries, key_rows, value_rows, grad_out,
        query_gain.reshape(1, HD), key_gain.reshape(1, HD), valid_frames, window_start,
    )
    row = jax.ShapeDtypeStruct((1, HD), f32)
    outs = pl.pallas_call(
        finish_kernel,
        out_shape=[slab] * 4 + [row] * 2,
        in_specs=[vmem_spec] * 5,
        out_specs=[any_spec] * 4 + [vmem_spec] * 2,
        scratch_shapes=[dma((4,))],
        compiler_params=pltpu.CompilerParams(vmem_limit_bytes=8 * 2**20),
        name="finish",
    )(*results)
    return (*outs[:4], outs[4].reshape(HD), outs[5].reshape(HD))


def solution(mesh):
    slabs = P("clip", "tm", None)
    return jax.shard_map(
        on_device,
        mesh=mesh,
        in_specs=(slabs,) * 4 + (P(), P(), P("clip", None), P("clip", None)),
        out_specs=(slabs,) * 4 + (P(), P()),
        check_vma=False,
    )
```

```python
import functools
import math

import jax
import jax.numpy as jnp
from jax import lax
from jax.experimental import pallas as pl
from jax.experimental.pallas import tpu as pltpu
from jax.sharding import PartitionSpec as P

MESH = pl.DeviceIdType.MESH
H = 12
HD = 128
GW = 4
WW = 2
TILE = 64
FRAME = 16
TOK = 256
HH = 1536
N_TM = 16
N_CLIP = 16
EPSILON = 1e-06
ROOT = 1.0 / math.sqrt(HD)
SCALE = ROOT * math.log2(math.e)
DEAD = -1e30
GROUPS = 6
PER = H // GROUPS
FULL = GROUPS - 1
PACKETS = FULL + PER

NT = (((1,), (1,)), ((), ()))
TN = (((0,), (0,)), ((), ()))


def dot(a, b, dims=(((1,), (0,)), ((), ()))):
    return lax.dot_general(a, b, dims, preferred_element_type=jnp.float32)


def cols(h):
    return pl.ds(pl.multiple_of(h * HD, HD), HD)


def packet_cols(n):
    if isinstance(n, int):
        first, count = (n * PER, PER) if n < FULL else (FULL * PER + n - FULL, 1)
        return pl.ds(first * HD, count * HD)
    return pl.ds(pl.multiple_of(n * PER * HD, PER * HD), PER * HD)


def inv_rms(values):
    return lax.rsqrt(jnp.mean(values * values, axis=-1, keepdims=True) + EPSILON)


def norm_back(values, scale, gain, upstream):
    weighted = gain * upstream
    inner = jnp.mean(values * weighted, axis=-1, keepdims=True)
    return scale * weighted - values * (scale * scale * scale * inner)


def fold(rows):
    return jnp.sum(rows.reshape(TOK // 8, 8, HD), axis=0)


def main_kernel(
    q_hbm, k_hbm, v_hbm, g_hbm, q_gain_any, k_gain_any, frames_any, starts_any,
    att_out, dq_out, dk_out, dv_out, gains_out,
    q_gain, k_gain, frames, starts, raw, halo, qn_own, kn_own, acc, stage, bias_f, bias_b,
    stat_cols, stat_mine, stat_halo, gain_acc, part, ring_in, clip_in, total,
    small_sem, load_sem, out_sem, send_sem, recv_sem, stat_send, stat_recv,
    ready, ring_send, ring_recv, clip_send, clip_recv, total_send, total_recv,
):
    me = lax.axis_index("tm")
    clip = lax.axis_index("clip")
    step = 1 - 2 * lax.rem(me, 2)
    near = me + step
    far = me - step
    has_far = jnp.logical_and(me > 0, me < N_TM - 1)
    sides = (near, far)
    middle = jnp.logical_or(me == N_TM // 2 - 1, me == N_TM // 2)
    loads = []
    for i, ref in enumerate((q_hbm, k_hbm, v_hbm, g_hbm)):
        load = pltpu.make_async_copy(ref.at[0], raw.at[i], load_sem.at[i])
        load.start()
        loads.append(load)

    small = []
    pairs = ((q_gain_any, q_gain), (k_gain_any, k_gain), (frames_any, frames), (starts_any, starts))
    for i, (source, target) in enumerate(pairs):
        load = pltpu.make_async_copy(source, target, small_sem.at[i])
        load.start()
        small.append(load)

    barrier = pltpu.get_barrier_semaphore()

    pl.semaphore_signal(barrier, inc=1, device_id={"tm": near}, device_id_type=MESH)

    @pl.when(has_far)
    def _():
        pl.semaphore_signal(barrier, inc=1, device_id={"tm": far}, device_id_type=MESH)

    @pl.when(me > 1)
    def _():
        pl.semaphore_signal(barrier, inc=1, device_id={"tm": 0}, device_id_type=MESH)

    @pl.when(me == 0)
    def _():
        for j in range(1, N_CLIP):
            pl.semaphore_signal(
                barrier, inc=1, device_id={"clip": lax.rem(clip + j, N_CLIP)}, device_id_type=MESH
            )
        pl.semaphore_wait(barrier, N_TM - 1 + N_CLIP - 1)
        for i in range(1, N_TM):
            pl.semaphore_signal(ready, inc=1, device_id={"tm": i}, device_id_type=MESH)

    @pl.when(has_far)
    def _():
        pl.semaphore_wait(barrier, 2)

    @pl.when(me == N_TM - 1)
    def _():
        pl.semaphore_wait(barrier, 1)

    def transfer(side, a, g):
        source = qn_own if a == 3 else (k_hbm, v_hbm, g_hbm)[a].at[0]
        return pltpu.make_async_remote_copy(
            src_ref=source.at[:, packet_cols(g)],
            dst_ref=halo.at[side, a, :, packet_cols(g)],
            send_sem=send_sem.at[side, a, g],
            recv_sem=recv_sem.at[side, a, g],
            device_id={"tm": sides[side]},
            device_id_type=MESH,
        )

    def stat_transfer(side, g):
        return pltpu.make_async_remote_copy(
            src_ref=stat_mine.at[g],
            dst_ref=stat_halo.at[side, g],
            send_sem=stat_send.at[side, g],
            recv_sem=stat_recv.at[side, g],
            device_id={"tm": sides[side]},
            device_id_type=MESH,
        )

    def send_near(a):
        for g in range(PACKETS):
            transfer(0, a, g).start()

    def send_far(arrays, g):
        @pl.when(has_far)
        def _():
            for a in arrays:
                transfer(1, a, g).start()

    def receive_near(arrays, g):
        for a in arrays:
            transfer(0, a, g).wait_recv()

    def receive_far(arrays, g):
        @pl.when(has_far)
        def _():
            for a in arrays:
                transfer(1, a, g).wait_recv()

    for g in range(PACKETS):
        send_far((0, 1), g)
    for a in (0, 1, 2):
        send_near(a)

    @pl.when(jnp.logical_not(has_far))
    def _():
        halo[1] = jnp.zeros((4, TOK, HH), jnp.bfloat16)
        stat_halo[1] = jnp.zeros((GROUPS, 8, TOK), jnp.float32)

    for load in small:
        load.wait()
    rows = lax.broadcasted_iota(jnp.int32, (TOK, TOK), 0)
    lanes = lax.broadcasted_iota(jnp.int32, (TOK, TOK), 1)

    def window_of(where, position, present):
        chosen = jnp.zeros((TOK, TOK), jnp.int32)
        for t in range(GW):
            start = starts[0, position * GW + t]
            chosen = jnp.where(where // TILE == t, jnp.where(present, start, -100), chosen)
        return chosen

    def bias_of(window, keys, count):
        column = keys // TILE
        frame = (keys % TILE) // FRAME
        live = (column >= window) & (column < window + WW) & (frame < count)
        return jnp.where(live, 0.0, DEAD).astype(jnp.float32)

    known = jnp.where(has_far, far, me)
    mine = window_of(rows, me, me >= 0)
    count_own = frames[0, me]
    bias_f[0] = bias_of(mine, lanes, frames[0, near])
    bias_f[1] = bias_of(mine, lanes, count_own)
    bias_f[2] = bias_of(mine, lanes, jnp.where(has_far, frames[0, known], 0))
    bias_b[0] = bias_of(window_of(lanes, near, me >= 0), rows, count_own)
    bias_b[1] = bias_of(window_of(lanes, known, has_far), rows, count_own)

    gain_acc[...] = jnp.zeros_like(gain_acc)
    stat_cols[...] = jnp.zeros_like(stat_cols)
    gain_q = q_gain[...]
    gain_k = k_gain[...]
    ungain_k = 1.0 / gain_k
    for load in loads:
        load.wait()

    def normal_queries(h, carry):
        values = raw[0, :, cols(h)].astype(jnp.float32)
        qn_own[:, cols(h)] = (values * inv_rms(values) * gain_q).astype(jnp.bfloat16)
        return carry

    lax.fori_loop(0, H, normal_queries, 0)
    send_far((2, 3), 0)

    @pl.when(middle)
    def _():
        send_far((2, 3), 1)

    send_near(3)

    stat_lane = lax.broadcasted_iota(jnp.int32, (TOK, HD), 1)

    def forward_head(local, g):
        h = g * PER + local
        at = cols(h)
        qn = qn_own[:, at]
        grads = raw[3, :, at]
        keys, extras, values = [], [], []
        for p in range(3):
            rough = (halo[0, 0, :, at], raw[1, :, at], halo[1, 0, :, at])[p].astype(jnp.float32)
            hat = rough * inv_rms(rough)
            kn = (hat * gain_k).astype(jnp.bfloat16)
            keys.append(kn)
            extras.append((hat - kn.astype(jnp.float32) * ungain_k).astype(jnp.bfloat16))
            values.append((halo[0, 1, :, at], raw[2, :, at], halo[1, 1, :, at])[p])
        kn_own[:, at] = keys[1]
        scores = [dot(qn, keys[p], NT) * SCALE + bias_f[p] for p in range(3)]
        peak = jnp.max(jnp.maximum(jnp.maximum(scores[0], scores[1]), scores[2]), axis=-1, keepdims=True)
        weights = [jnp.exp2(s - peak) for s in scores]
        mass = jnp.sum(weights[0] + weights[1] + weights[2], axis=-1, keepdims=True)
        inverse = 1.0 / mass
        probs = [w * inverse for w in weights]
        slopes = [dot(grads, values[p], NT) for p in range(3)]
        delta = jnp.sum(
            probs[0] * slopes[0] + probs[1] * slopes[1] + probs[2] * slopes[2], axis=-1, keepdims=True
        )
        low = [x.astype(jnp.bfloat16) for x in probs]
        change = [(probs[p] * (slopes[p] - delta)).astype(jnp.bfloat16) for p in range(3)]
        stage[0, :, at] = sum(dot(low[p], values[p]) for p in range(3)).astype(jnp.bfloat16)
        wide = sum(
            dot(change[p], jnp.concatenate([keys[p], extras[p]], axis=1)) for p in range(3)
        )
        dqn = wide[:, :HD] * ROOT
        by_hat = dqn * ungain_k + wide[:, HD:] * ROOT
        query = raw[0, :, at].astype(jnp.float32)
        scale = inv_rms(query)
        gain_acc[0] += fold(dqn * query * scale)
        gain_acc[1] += fold(qn.astype(jnp.float32) * by_hat)
        stage[1, :, at] = norm_back(query, scale, gain_q, dqn).astype(jnp.bfloat16)
        acc[0, :, at] = dot(change[1], qn, TN)
        acc[1, :, at] = dot(low[1], grads, TN)
        logs = peak + jnp.log2(mass)
        kept = stat_cols[...]
        kept = jnp.where(stat_lane == 2 * local, logs, kept)
        stat_cols[...] = jnp.where(stat_lane == 2 * local + 1, delta, kept)
        return g

    def out_copy(ref, i, g):
        return pltpu.make_async_copy(
            stage.at[i, :, packet_cols(g)], ref.at[0, :, packet_cols(g)], out_sem.at[i, g]
        )

    def keep_stats(g):
        stat_mine[g] = jnp.transpose(stat_cols[...])[:8]
        stat_transfer(0, g).start()

        @pl.when(has_far)
        def _():
            stat_transfer(1, g).start()

    def forward_group(g, carry):
        receive_near((0, 1), g)
        receive_far((0, 1), g)
        lax.fori_loop(0, PER, forward_head, g, unroll=True)
        keep_stats(g)
        out_copy(att_out, 0, g).start()
        out_copy(dq_out, 1, g).start()
        return carry

    lax.fori_loop(0, FULL, forward_group, 0)
    for local in range(PER):
        receive_near((0, 1), FULL + local)
        receive_far((0, 1), FULL + local)
        forward_head(local, FULL)

    row8 = lax.broadcasted_iota(jnp.int32, (8, HD), 0)
    query_part = jnp.sum(gain_acc[0], axis=0, keepdims=True)
    key_part = jnp.sum(gain_acc[1], axis=0, keepdims=True)
    part[...] = jnp.where(row8 == 0, query_part, jnp.where(row8 == 1, key_part, 0.0))

    def to_ring(i):
        return pltpu.make_async_remote_copy(
            src_ref=part, dst_ref=ring_in.at[i], send_sem=ring_send, recv_sem=ring_recv.at[i],
            device_id={"tm": 0}, device_id_type=MESH,
        )

    @pl.when(me > 0)
    def _():
        pl.semaphore_wait(ready, 1)
        to_ring(me).start()

    keep_stats(FULL)

    @pl.when(jnp.logical_not(middle))
    def _():
        send_far((2, 3), 1)

    for g in range(2, PACKETS):
        send_far((2, 3), g)

    for n in range(FULL, PACKETS):
        out_copy(att_out, 0, n).start()
        out_copy(dq_out, 1, n).start()

    def to_clip(j, slot):
        return pltpu.make_async_remote_copy(
            src_ref=clip_in.at[clip], dst_ref=clip_in.at[slot], send_sem=clip_send.at[j],
            recv_sem=clip_recv.at[slot], device_id={"clip": lax.rem(clip + j, N_CLIP)},
            device_id_type=MESH,
        )

    def to_all(i):
        return pltpu.make_async_remote_copy(
            src_ref=total, dst_ref=total, send_sem=total_send.at[i], recv_sem=total_recv,
            device_id={"tm": i}, device_id_type=MESH,
        )

    @pl.when(me == 0)
    def _():
        ring = part[...]
        for i in range(1, N_TM):
            to_ring(i).wait_recv()
            ring = ring + ring_in[i]
        clip_in[clip] = ring
        for j in range(1, N_CLIP):
            to_clip(j, clip).start()

    def share_total():
        for j in range(1, N_CLIP):
            to_clip(j, lax.rem(clip + j, N_CLIP)).wait_recv()
        everything = clip_in[0]
        for c in range(1, N_CLIP):
            everything = everything + clip_in[c]
        total[...] = everything
        for i in range(1, N_TM):
            to_all(i).start()

    def backward_terms(side, local, g):
        at = cols(g * PER + local)
        qn = halo[side, 3, :, at]
        grads = halo[side, 2, :, at]
        logs = stat_halo[side, g, pl.ds(2 * local, 1), :]
        delta = stat_halo[side, g, pl.ds(2 * local + 1, 1), :]
        probs = jnp.exp2(dot(kn_own[:, at], qn, NT) * SCALE + bias_b[side] - logs)
        slopes = dot(raw[2, :, at], grads, NT)
        change = (probs * (slopes - delta)).astype(jnp.bfloat16)
        return (
            acc[0, :, at] + dot(change, qn),
            acc[1, :, at] + dot(probs.astype(jnp.bfloat16), grads),
        )

    def near_head(local, g):
        at = cols(g * PER + local)
        dk, dv = backward_terms(0, local, g)
        acc[0, :, at] = dk
        acc[1, :, at] = dv
        return g

    def far_head(local, g):
        at = cols(g * PER + local)
        dk, dv = backward_terms(1, local, g)
        rough = raw[1, :, at].astype(jnp.float32)
        stage[2, :, at] = norm_back(rough, inv_rms(rough), gain_k, dk * ROOT).astype(jnp.bfloat16)
        stage[3, :, at] = dv.astype(jnp.bfloat16)
        return g

    def backward_group(g, carry):
        stat_transfer(0, g).wait_recv()
        receive_near((2, 3), g)
        lax.fori_loop(0, PER, near_head, g, unroll=True)

        @pl.when(has_far)
        def _():
            stat_transfer(1, g).wait_recv()

        receive_far((2, 3), g)

        lax.fori_loop(0, PER, far_head, g, unroll=True)
        out_copy(dk_out, 2, g).start()
        out_copy(dv_out, 3, g).start()
        return carry

    lax.fori_loop(0, FULL, backward_group, 0)
    stat_transfer(0, FULL).wait_recv()
    for local in range(PER):
        receive_near((2, 3), FULL + local)
        near_head(local, FULL)

    @pl.when(has_far)
    def _():
        stat_transfer(1, FULL).wait_recv()

    for local in range(PER):
        receive_far((2, 3), FULL + local)
        far_head(local, FULL)
        out_copy(dk_out, 2, FULL + local).start()
        out_copy(dv_out, 3, FULL + local).start()

    @pl.when(me == 0)
    def _():
        share_total()


    @pl.when(me > 0)
    def _():
        to_all(0).wait_recv()
        to_ring(me).wait_send()

    @pl.when(me == 0)
    def _():
        for j in range(1, N_CLIP):
            to_clip(j, clip).wait_send()
        for i in range(1, N_TM):
            to_all(i).wait_send()

    gains_out[...] = total[...]
    def all_sent(side):
        for n in range(PACKETS):
            for a in range(4):
                transfer(side, a, n).wait_send()
        for g in range(GROUPS):
            stat_transfer(side, g).wait_send()

    all_sent(0)

    @pl.when(has_far)
    def _():
        all_sent(1)

    for i, ref in enumerate((att_out, dq_out, dk_out, dv_out)):
        for n in range(PACKETS):
            out_copy(ref, i, n).wait()


def finish_kernel(*refs):
    ins, gains, outs, q_total, k_total = refs[:4], refs[4], refs[5:9], refs[9], refs[10]
    out_sem = refs[11]
    writes = [pltpu.make_async_copy(ins[i], outs[i], out_sem.at[i]) for i in range(4)]
    for write in writes:
        write.start()
    q_total[...] = gains[0:1]
    k_total[...] = gains[1:2]
    for write in writes:
        write.wait()


def on_device(
    queries, key_rows, value_rows, grad_out, query_gain, key_gain, valid_frames, window_start
):
    any_spec = pl.BlockSpec(memory_space=pl.ANY)
    vmem_spec = pl.BlockSpec(memory_space=pltpu.VMEM)
    slab = jax.ShapeDtypeStruct((1, TOK, HH), jnp.bfloat16)
    dma = pltpu.SemaphoreType.DMA
    bf16, f32 = jnp.bfloat16, jnp.float32
    results = pl.pallas_call(
        main_kernel,
        out_shape=[slab] * 4 + [jax.ShapeDtypeStruct((8, HD), f32)],
        in_specs=[any_spec] * 8,
        out_specs=[any_spec] * 4 + [vmem_spec],
        scratch_shapes=[
            pltpu.VMEM((1, HD), f32),
            pltpu.VMEM((1, HD), f32),
            pltpu.SMEM((1, N_TM), jnp.int32),
            pltpu.SMEM((1, N_TM * GW), jnp.int32),
            pltpu.VMEM((4, TOK, HH), bf16),
            pltpu.VMEM((2, 4, TOK, HH), bf16),
            pltpu.VMEM((TOK, HH), bf16),
            pltpu.VMEM((TOK, HH), bf16),
            pltpu.VMEM((2, TOK, HH), f32),
            pltpu.VMEM((4, TOK, HH), bf16),
            pltpu.VMEM((3, TOK, TOK), f32),
            pltpu.VMEM((2, TOK, TOK), f32),
            pltpu.VMEM((TOK, HD), f32),
            pltpu.VMEM((GROUPS, 8, TOK), f32),
            pltpu.VMEM((2, GROUPS, 8, TOK), f32),
            pltpu.VMEM((2, 8, HD), f32),
            pltpu.VMEM((8, HD), f32),
            pltpu.VMEM((N_TM, 8, HD), f32),
            pltpu.VMEM((N_CLIP, 8, HD), f32),
            pltpu.VMEM((8, HD), f32),
            dma((4,)),
            dma((4,)),
            dma((4, PACKETS)),
            dma((2, 4, PACKETS)),
            dma((2, 4, PACKETS)),
            dma((2, GROUPS)),
            dma((2, GROUPS)),
            pltpu.SemaphoreType.REGULAR,
            dma,
            dma((N_TM,)),
            dma((N_CLIP,)),
            dma((N_CLIP,)),
            dma((N_TM,)),
            dma,
        ],
        compiler_params=pltpu.CompilerParams(
            collective_id=0, has_side_effects=True, vmem_limit_bytes=203 * 2**18
        ),
        name="attend",
    )(
        queries, key_rows, value_rows, grad_out,
        query_gain.reshape(1, HD), key_gain.reshape(1, HD), valid_frames, window_start,
    )
    row = jax.ShapeDtypeStruct((1, HD), f32)
    outs = pl.pallas_call(
        finish_kernel,
        out_shape=[slab] * 4 + [row] * 2,
        in_specs=[vmem_spec] * 5,
        out_specs=[any_spec] * 4 + [vmem_spec] * 2,
        scratch_shapes=[dma((4,))],
        compiler_params=pltpu.CompilerParams(vmem_limit_bytes=8 * 2**20),
        name="finish",
    )(*results)
    return (*outs[:4], outs[4].reshape(HD), outs[5].reshape(HD))


def solution(mesh):
    slabs = P("clip", "tm", None)
    return jax.shard_map(
        on_device,
        mesh=mesh,
        in_specs=(slabs,) * 4 + (P(), P(), P("clip", None), P("clip", None)),
        out_specs=(slabs,) * 4 + (P(), P()),
        check_vma=False,
    )
```

```python
import functools
import math

import jax
import jax.numpy as jnp
from jax import lax
from jax.experimental import pallas as pl
from jax.experimental.pallas import tpu as pltpu
from jax.sharding import PartitionSpec as P

MESH = pl.DeviceIdType.MESH
H = 12
HD = 128
GW = 4
WW = 2
TILE = 64
FRAME = 16
TOK = 256
HH = 1536
N_TM = 16
N_CLIP = 16
EPSILON = 1e-06
ROOT = 1.0 / math.sqrt(HD)
SCALE = ROOT * math.log2(math.e)
DEAD = -1e30
GROUPS = 6
PER = H // GROUPS
FULL = GROUPS - 1
PACKETS = FULL + PER

NT = (((1,), (1,)), ((), ()))
TN = (((0,), (0,)), ((), ()))


def dot(a, b, dims=(((1,), (0,)), ((), ()))):
    return lax.dot_general(a, b, dims, preferred_element_type=jnp.float32)


def cols(h):
    return pl.ds(pl.multiple_of(h * HD, HD), HD)


def packet_cols(n):
    if isinstance(n, int):
        first, count = (n * PER, PER) if n < FULL else (FULL * PER + n - FULL, 1)
        return pl.ds(first * HD, count * HD)
    return pl.ds(pl.multiple_of(n * PER * HD, PER * HD), PER * HD)


def inv_rms(values):
    return lax.rsqrt(jnp.mean(values * values, axis=-1, keepdims=True) + EPSILON)


def norm_back(values, scale, gain, upstream):
    weighted = gain * upstream
    inner = jnp.mean(values * weighted, axis=-1, keepdims=True)
    return scale * weighted - values * (scale * scale * scale * inner)


def fold(rows):
    return jnp.sum(rows.reshape(TOK // 8, 8, HD), axis=0)


def main_kernel(
    q_hbm, k_hbm, v_hbm, g_hbm, q_gain_any, k_gain_any, frames_any, starts_any,
    att_out, dq_out, dk_out, dv_out, gains_out,
    q_gain, k_gain, frames, starts, raw, halo, qn_own, kn_own, acc, stage, bias_f, bias_b,
    stat_cols, stat_mine, stat_halo, gain_acc, part, ring_in, clip_in, total,
    small_sem, load_sem, out_sem, send_sem, recv_sem, stat_send, stat_recv,
    ready, ring_send, ring_recv, clip_send, clip_recv, total_send, total_recv,
):
    me = lax.axis_index("tm")
    clip = lax.axis_index("clip")
    step = 1 - 2 * lax.rem(me, 2)
    near = me + step
    far = me - step
    has_far = jnp.logical_and(me > 0, me < N_TM - 1)
    sides = (near, far)
    middle = jnp.logical_or(me == N_TM // 2 - 1, me == N_TM // 2)
    barrier = pltpu.get_barrier_semaphore()

    pl.semaphore_signal(barrier, inc=1, device_id={"tm": near}, device_id_type=MESH)

    @pl.when(has_far)
    def _():
        pl.semaphore_signal(barrier, inc=1, device_id={"tm": far}, device_id_type=MESH)

    @pl.when(me > 1)
    def _():
        pl.semaphore_signal(barrier, inc=1, device_id={"tm": 0}, device_id_type=MESH)

    loads = []
    for i, ref in enumerate((q_hbm, k_hbm, v_hbm, g_hbm)):
        load = pltpu.make_async_copy(ref.at[0], raw.at[i], load_sem.at[i])
        load.start()
        loads.append(load)

    small = []
    pairs = ((q_gain_any, q_gain), (k_gain_any, k_gain), (frames_any, frames), (starts_any, starts))
    for i, (source, target) in enumerate(pairs):
        load = pltpu.make_async_copy(source, target, small_sem.at[i])
        load.start()
        small.append(load)

    @pl.when(me == 0)
    def _():
        for j in range(1, N_CLIP):
            pl.semaphore_signal(
                barrier, inc=1, device_id={"clip": lax.rem(clip + j, N_CLIP)}, device_id_type=MESH
            )
        pl.semaphore_wait(barrier, N_TM - 1 + N_CLIP - 1)
        for i in range(1, N_TM):
            pl.semaphore_signal(ready, inc=1, device_id={"tm": i}, device_id_type=MESH)

    @pl.when(has_far)
    def _():
        pl.semaphore_wait(barrier, 2)

    @pl.when(me == N_TM - 1)
    def _():
        pl.semaphore_wait(barrier, 1)

    def transfer(side, a, g):
        source = qn_own if a == 3 else (k_hbm, v_hbm, g_hbm)[a].at[0]
        return pltpu.make_async_remote_copy(
            src_ref=source.at[:, packet_cols(g)],
            dst_ref=halo.at[side, a, :, packet_cols(g)],
            send_sem=send_sem.at[side, a, g],
            recv_sem=recv_sem.at[side, a, g],
            device_id={"tm": sides[side]},
            device_id_type=MESH,
        )

    def stat_transfer(side, g):
        return pltpu.make_async_remote_copy(
            src_ref=stat_mine.at[g],
            dst_ref=stat_halo.at[side, g],
            send_sem=stat_send.at[side, g],
            recv_sem=stat_recv.at[side, g],
            device_id={"tm": sides[side]},
            device_id_type=MESH,
        )

    def send_near(a):
        for g in range(PACKETS):
            transfer(0, a, g).start()

    def send_far(arrays, g):
        @pl.when(has_far)
        def _():
            for a in arrays:
                transfer(1, a, g).start()

    def receive_near(arrays, g):
        for a in arrays:
            transfer(0, a, g).wait_recv()

    def receive_far(arrays, g):
        @pl.when(has_far)
        def _():
            for a in arrays:
                transfer(1, a, g).wait_recv()

    for g in range(PACKETS):
        send_far((0, 1), g)
    for a in (0, 1, 2):
        send_near(a)

    @pl.when(jnp.logical_not(has_far))
    def _():
        halo[1] = jnp.zeros((4, TOK, HH), jnp.bfloat16)
        stat_halo[1] = jnp.zeros((GROUPS, 8, TOK), jnp.float32)

    for load in small:
        load.wait()
    rows = lax.broadcasted_iota(jnp.int32, (TOK, TOK), 0)
    lanes = lax.broadcasted_iota(jnp.int32, (TOK, TOK), 1)

    def window_of(where, position, present):
        chosen = jnp.zeros((TOK, TOK), jnp.int32)
        for t in range(GW):
            start = starts[0, position * GW + t]
            chosen = jnp.where(where // TILE == t, jnp.where(present, start, -100), chosen)
        return chosen

    def bias_of(window, keys, count):
        column = keys // TILE
        frame = (keys % TILE) // FRAME
        live = (column >= window) & (column < window + WW) & (frame < count)
        return jnp.where(live, 0.0, DEAD).astype(jnp.float32)

    known = jnp.where(has_far, far, me)
    mine = window_of(rows, me, me >= 0)
    count_own = frames[0, me]
    bias_f[0] = bias_of(mine, lanes, frames[0, near])
    bias_f[1] = bias_of(mine, lanes, count_own)
    bias_f[2] = bias_of(mine, lanes, jnp.where(has_far, frames[0, known], 0))
    bias_b[0] = bias_of(window_of(lanes, near, me >= 0), rows, count_own)
    bias_b[1] = bias_of(window_of(lanes, known, has_far), rows, count_own)

    gain_acc[...] = jnp.zeros_like(gain_acc)
    stat_cols[...] = jnp.zeros_like(stat_cols)
    gain_q = q_gain[...]
    gain_k = k_gain[...]
    ungain_k = 1.0 / gain_k
    for load in loads:
        load.wait()

    def normal_queries(h, carry):
        values = raw[0, :, cols(h)].astype(jnp.float32)
        qn_own[:, cols(h)] = (values * inv_rms(values) * gain_q).astype(jnp.bfloat16)
        return carry

    lax.fori_loop(0, H, normal_queries, 0)
    send_far((2, 3), 0)

    @pl.when(middle)
    def _():
        send_far((2,), 1)

    send_near(3)

    stat_lane = lax.broadcasted_iota(jnp.int32, (TOK, HD), 1)

    def forward_head(local, g):
        h = g * PER + local
        at = cols(h)
        qn = qn_own[:, at]
        grads = raw[3, :, at]
        keys, extras, values = [], [], []
        for p in range(3):
            rough = (halo[0, 0, :, at], raw[1, :, at], halo[1, 0, :, at])[p].astype(jnp.float32)
            hat = rough * inv_rms(rough)
            kn = (hat * gain_k).astype(jnp.bfloat16)
            keys.append(kn)
            extras.append((hat - kn.astype(jnp.float32) * ungain_k).astype(jnp.bfloat16))
            values.append((halo[0, 1, :, at], raw[2, :, at], halo[1, 1, :, at])[p])
        kn_own[:, at] = keys[1]
        scores = [dot(qn, keys[p], NT) * SCALE + bias_f[p] for p in range(3)]
        peak = jnp.max(jnp.maximum(jnp.maximum(scores[0], scores[1]), scores[2]), axis=-1, keepdims=True)
        weights = [jnp.exp2(s - peak) for s in scores]
        mass = jnp.sum(weights[0] + weights[1] + weights[2], axis=-1, keepdims=True)
        inverse = 1.0 / mass
        probs = [w * inverse for w in weights]
        slopes = [dot(grads, values[p], NT) for p in range(3)]
        delta = jnp.sum(
            probs[0] * slopes[0] + probs[1] * slopes[1] + probs[2] * slopes[2], axis=-1, keepdims=True
        )
        low = [x.astype(jnp.bfloat16) for x in probs]
        change = [(probs[p] * (slopes[p] - delta)).astype(jnp.bfloat16) for p in range(3)]
        stage[0, :, at] = sum(dot(low[p], values[p]) for p in range(3)).astype(jnp.bfloat16)
        wide = sum(
            dot(change[p], jnp.concatenate([keys[p], extras[p]], axis=1)) for p in range(3)
        )
        dqn = wide[:, :HD] * ROOT
        by_hat = dqn * ungain_k + wide[:, HD:] * ROOT
        query = raw[0, :, at].astype(jnp.float32)
        scale = inv_rms(query)
        gain_acc[0] += fold(dqn * query * scale)
        gain_acc[1] += fold(qn.astype(jnp.float32) * by_hat)
        stage[1, :, at] = norm_back(query, scale, gain_q, dqn).astype(jnp.bfloat16)
        acc[0, :, at] = dot(change[1], qn, TN)
        acc[1, :, at] = dot(low[1], grads, TN)
        logs = peak + jnp.log2(mass)
        kept = stat_cols[...]
        kept = jnp.where(stat_lane == 2 * local, logs, kept)
        stat_cols[...] = jnp.where(stat_lane == 2 * local + 1, delta, kept)
        return g

    def out_copy(ref, i, g):
        return pltpu.make_async_copy(
            stage.at[i, :, packet_cols(g)], ref.at[0, :, packet_cols(g)], out_sem.at[i, g]
        )

    def keep_stats(g):
        stat_mine[g] = jnp.transpose(stat_cols[...])[:8]
        stat_transfer(0, g).start()

        @pl.when(has_far)
        def _():
            stat_transfer(1, g).start()

    def forward_group(g, carry):
        receive_near((0, 1), g)
        receive_far((0, 1), g)
        lax.fori_loop(0, PER, forward_head, g, unroll=True)
        keep_stats(g)
        out_copy(att_out, 0, g).start()
        out_copy(dq_out, 1, g).start()
        return carry

    lax.fori_loop(0, FULL, forward_group, 0)
    for local in range(PER):
        receive_near((0, 1), FULL + local)
        receive_far((0, 1), FULL + local)
        forward_head(local, FULL)

    row8 = lax.broadcasted_iota(jnp.int32, (8, HD), 0)
    query_part = jnp.sum(gain_acc[0], axis=0, keepdims=True)
    key_part = jnp.sum(gain_acc[1], axis=0, keepdims=True)
    part[...] = jnp.where(row8 == 0, query_part, jnp.where(row8 == 1, key_part, 0.0))

    def to_ring(i):
        return pltpu.make_async_remote_copy(
            src_ref=part, dst_ref=ring_in.at[i], send_sem=ring_send, recv_sem=ring_recv.at[i],
            device_id={"tm": 0}, device_id_type=MESH,
        )

    @pl.when(me > 0)
    def _():
        pl.semaphore_wait(ready, 1)
        to_ring(me).start()

    keep_stats(FULL)

    @pl.when(jnp.logical_not(middle))
    def _():
        send_far((2,), 1)

    send_far((3,), 1)

    for g in range(2, PACKETS):
        send_far((2, 3), g)

    for n in range(FULL, PACKETS):
        out_copy(att_out, 0, n).start()
        out_copy(dq_out, 1, n).start()

    def to_clip(c, slot):
        return pltpu.make_async_remote_copy(
            src_ref=clip_in.at[clip], dst_ref=clip_in.at[slot], send_sem=clip_send.at[c],
            recv_sem=clip_recv.at[slot], device_id={"clip": c},
            device_id_type=MESH,
        )

    def to_all(i):
        return pltpu.make_async_remote_copy(
            src_ref=total, dst_ref=total, send_sem=total_send.at[i], recv_sem=total_recv,
            device_id={"tm": i}, device_id_type=MESH,
        )

    @pl.when(me == 0)
    def _():
        ring = part[...]
        for i in range(1, N_TM):
            to_ring(i).wait_recv()
            ring = ring + ring_in[i]
        clip_in[clip] = ring
        for c in range(N_CLIP):

            @pl.when(clip != c)
            def _():
                to_clip(c, clip).start()

    def share_total():
        for c in range(N_CLIP):

            @pl.when(clip != c)
            def _():
                to_clip(c, c).wait_recv()

        everything = clip_in[0]
        for c in range(1, N_CLIP):
            everything = everything + clip_in[c]
        total[...] = everything
        for i in range(1, N_TM):
            to_all(i).start()

    def backward_terms(side, local, g):
        at = cols(g * PER + local)
        qn = halo[side, 3, :, at]
        grads = halo[side, 2, :, at]
        logs = stat_halo[side, g, pl.ds(2 * local, 1), :]
        delta = stat_halo[side, g, pl.ds(2 * local + 1, 1), :]
        probs = jnp.exp2(dot(kn_own[:, at], qn, NT) * SCALE + bias_b[side] - logs)
        slopes = dot(raw[2, :, at], grads, NT)
        change = (probs * (slopes - delta)).astype(jnp.bfloat16)
        return (
            acc[0, :, at] + dot(change, qn),
            acc[1, :, at] + dot(probs.astype(jnp.bfloat16), grads),
        )

    def near_head(local, g):
        at = cols(g * PER + local)
        dk, dv = backward_terms(0, local, g)
        acc[0, :, at] = dk
        acc[1, :, at] = dv
        return g

    def far_head(local, g):
        at = cols(g * PER + local)
        dk, dv = backward_terms(1, local, g)
        rough = raw[1, :, at].astype(jnp.float32)
        stage[2, :, at] = norm_back(rough, inv_rms(rough), gain_k, dk * ROOT).astype(jnp.bfloat16)
        stage[3, :, at] = dv.astype(jnp.bfloat16)
        return g

    def backward_group(g, carry):
        stat_transfer(0, g).wait_recv()
        receive_near((2, 3), g)
        lax.fori_loop(0, PER, near_head, g, unroll=True)

        @pl.when(has_far)
        def _():
            stat_transfer(1, g).wait_recv()

        receive_far((2, 3), g)

        lax.fori_loop(0, PER, far_head, g, unroll=True)
        out_copy(dk_out, 2, g).start()
        out_copy(dv_out, 3, g).start()
        return carry

    lax.fori_loop(0, FULL, backward_group, 0)
    stat_transfer(0, FULL).wait_recv()
    for local in range(PER):
        receive_near((2, 3), FULL + local)
        near_head(local, FULL)

    def all_sent(side, arrays):
        for n in range(PACKETS):
            for a in arrays:
                transfer(side, a, n).wait_send()

    all_sent(0, (0, 1, 2, 3))
    for g in range(GROUPS):
        stat_transfer(0, g).wait_send()

    @pl.when(has_far)
    def _():
        all_sent(1, (0, 1))
        for g in range(GROUPS):
            stat_transfer(1, g).wait_send()
        stat_transfer(1, FULL).wait_recv()

    @pl.when(me > 0)
    def _():
        to_ring(me).wait_send()

    for n in range(PACKETS):
        out_copy(att_out, 0, n).wait()
        out_copy(dq_out, 1, n).wait()
    for n in range(FULL):
        out_copy(dk_out, 2, n).wait()
        out_copy(dv_out, 3, n).wait()

    for local in range(PER):
        receive_far((2, 3), FULL + local)
        far_head(local, FULL)
        out_copy(dk_out, 2, FULL + local).start()
        out_copy(dv_out, 3, FULL + local).start()

    @pl.when(me == 0)
    def _():
        share_total()

    @pl.when(has_far)
    def _():
        all_sent(1, (2, 3))

    for n in range(FULL, PACKETS):
        out_copy(dk_out, 2, n).wait()
        out_copy(dv_out, 3, n).wait()

    @pl.when(me == 0)
    def _():
        for c in range(N_CLIP):

            @pl.when(clip != c)
            def _():
                to_clip(c, clip).wait_send()

        for i in range(1, N_TM):
            to_all(i).wait_send()

    @pl.when(me > 0)
    def _():
        to_all(0).wait_recv()

    gains_out[...] = total[...]


def finish_kernel(*refs):
    ins, gains, outs, q_total, k_total = refs[:4], refs[4], refs[5:9], refs[9], refs[10]
    out_sem = refs[11]
    writes = [pltpu.make_async_copy(ins[i], outs[i], out_sem.at[i]) for i in range(4)]
    for write in writes:
        write.start()
    q_total[...] = gains[0:1]
    k_total[...] = gains[1:2]
    for write in writes:
        write.wait()


def on_device(
    queries, key_rows, value_rows, grad_out, query_gain, key_gain, valid_frames, window_start
):
    any_spec = pl.BlockSpec(memory_space=pl.ANY)
    vmem_spec = pl.BlockSpec(memory_space=pltpu.VMEM)
    slab = jax.ShapeDtypeStruct((1, TOK, HH), jnp.bfloat16)
    dma = pltpu.SemaphoreType.DMA
    bf16, f32 = jnp.bfloat16, jnp.float32
    results = pl.pallas_call(
        main_kernel,
        out_shape=[slab] * 4 + [jax.ShapeDtypeStruct((8, HD), f32)],
        in_specs=[any_spec] * 8,
        out_specs=[any_spec] * 4 + [vmem_spec],
        scratch_shapes=[
            pltpu.VMEM((1, HD), f32),
            pltpu.VMEM((1, HD), f32),
            pltpu.SMEM((1, N_TM), jnp.int32),
            pltpu.SMEM((1, N_TM * GW), jnp.int32),
            pltpu.VMEM((4, TOK, HH), bf16),
            pltpu.VMEM((2, 4, TOK, HH), bf16),
            pltpu.VMEM((TOK, HH), bf16),
            pltpu.VMEM((TOK, HH), bf16),
            pltpu.VMEM((2, TOK, HH), f32),
            pltpu.VMEM((4, TOK, HH), bf16),
            pltpu.VMEM((3, TOK, TOK), f32),
            pltpu.VMEM((2, TOK, TOK), f32),
            pltpu.VMEM((TOK, HD), f32),
            pltpu.VMEM((GROUPS, 8, TOK), f32),
            pltpu.VMEM((2, GROUPS, 8, TOK), f32),
            pltpu.VMEM((2, 8, HD), f32),
            pltpu.VMEM((8, HD), f32),
            pltpu.VMEM((N_TM, 8, HD), f32),
            pltpu.VMEM((N_CLIP, 8, HD), f32),
            pltpu.VMEM((8, HD), f32),
            dma((4,)),
            dma((4,)),
            dma((4, PACKETS)),
            dma((2, 4, PACKETS)),
            dma((2, 4, PACKETS)),
            dma((2, GROUPS)),
            dma((2, GROUPS)),
            pltpu.SemaphoreType.REGULAR,
            dma,
            dma((N_TM,)),
            dma((N_CLIP,)),
            dma((N_CLIP,)),
            dma((N_TM,)),
            dma,
        ],
        compiler_params=pltpu.CompilerParams(
            collective_id=0, has_side_effects=True, vmem_limit_bytes=203 * 2**18
        ),
        name="attend",
    )(
        queries, key_rows, value_rows, grad_out,
        query_gain.reshape(1, HD), key_gain.reshape(1, HD), valid_frames, window_start,
    )
    row = jax.ShapeDtypeStruct((1, HD), f32)
    outs = pl.pallas_call(
        finish_kernel,
        out_shape=[slab] * 4 + [row] * 2,
        in_specs=[vmem_spec] * 5,
        out_specs=[any_spec] * 4 + [vmem_spec] * 2,
        scratch_shapes=[dma((4,))],
        compiler_params=pltpu.CompilerParams(vmem_limit_bytes=8 * 2**20),
        name="finish",
    )(*results)
    return (*outs[:4], outs[4].reshape(HD), outs[5].reshape(HD))


def solution(mesh):
    slabs = P("clip", "tm", None)
    return jax.shard_map(
        on_device,
        mesh=mesh,
        in_specs=(slabs,) * 4 + (P(), P(), P("clip", None), P("clip", None)),
        out_specs=(slabs,) * 4 + (P(), P()),
        check_vma=False,
    )
```

```python
import functools
import math

import jax
import jax.numpy as jnp
from jax import lax
from jax.experimental import pallas as pl
from jax.experimental.pallas import tpu as pltpu
from jax.sharding import PartitionSpec as P

MESH = pl.DeviceIdType.MESH
H = 12
HD = 128
GW = 4
WW = 2
TILE = 64
FRAME = 16
TOK = 256
HH = 1536
N_TM = 16
N_CLIP = 16
EPSILON = 1e-06
ROOT = 1.0 / math.sqrt(HD)
SCALE = ROOT * math.log2(math.e)
DEAD = -1e30
GROUPS = 6
PER = H // GROUPS
FULL = GROUPS - 1
PACKETS = FULL + PER

NT = (((1,), (1,)), ((), ()))
TN = (((0,), (0,)), ((), ()))


def dot(a, b, dims=(((1,), (0,)), ((), ()))):
    return lax.dot_general(a, b, dims, preferred_element_type=jnp.float32)


def cols(h):
    return pl.ds(pl.multiple_of(h * HD, HD), HD)


def packet_cols(n):
    if isinstance(n, int):
        first, count = (n * PER, PER) if n < FULL else (FULL * PER + n - FULL, 1)
        return pl.ds(first * HD, count * HD)
    return pl.ds(pl.multiple_of(n * PER * HD, PER * HD), PER * HD)


def inv_rms(values):
    return lax.rsqrt(jnp.mean(values * values, axis=-1, keepdims=True) + EPSILON)


def norm_back(values, scale, gain, upstream):
    weighted = gain * upstream
    inner = jnp.mean(values * weighted, axis=-1, keepdims=True)
    return scale * weighted - values * (scale * scale * scale * inner)


def fold(rows):
    return jnp.sum(rows.reshape(TOK // 8, 8, HD), axis=0)


def main_kernel(
    q_hbm, k_hbm, v_hbm, g_hbm, q_gain_any, k_gain_any, frames_any, starts_any,
    att_out, dq_out, dk_out, dv_out, gains_out,
    q_gain, k_gain, frames, starts, raw, halo, qn_own, kn_own, acc, stage, bias_f, bias_b,
    stat_cols, stat_mine, stat_halo, gain_acc, part, ring_in, clip_in, total,
    small_sem, load_sem, out_sem, send_sem, recv_sem, stat_send, stat_recv,
    ready, ring_send, ring_recv, clip_send, clip_recv, total_send, total_recv, own_sem,
):
    me = lax.axis_index("tm")
    clip = lax.axis_index("clip")
    step = 1 - 2 * lax.rem(me, 2)
    near = me + step
    far = me - step
    has_far = jnp.logical_and(me > 0, me < N_TM - 1)
    sides = (near, far)
    middle = jnp.logical_or(me == N_TM // 2 - 1, me == N_TM // 2)
    barrier = pltpu.get_barrier_semaphore()

    pl.semaphore_signal(barrier, inc=1, device_id={"tm": near}, device_id_type=MESH)

    @pl.when(has_far)
    def _():
        pl.semaphore_signal(barrier, inc=1, device_id={"tm": far}, device_id_type=MESH)

    @pl.when(me > 1)
    def _():
        pl.semaphore_signal(barrier, inc=1, device_id={"tm": 0}, device_id_type=MESH)

    loads = []
    for i, ref in enumerate((q_hbm, k_hbm, v_hbm, g_hbm)):
        load = pltpu.make_async_copy(ref.at[0], raw.at[i], load_sem.at[i])
        load.start()
        loads.append(load)

    small = []
    pairs = ((q_gain_any, q_gain), (k_gain_any, k_gain), (frames_any, frames), (starts_any, starts))
    for i, (source, target) in enumerate(pairs):
        load = pltpu.make_async_copy(source, target, small_sem.at[i])
        load.start()
        small.append(load)

    @pl.when(me == 0)
    def _():
        for j in range(1, N_CLIP):
            pl.semaphore_signal(
                barrier, inc=1, device_id={"clip": lax.rem(clip + j, N_CLIP)}, device_id_type=MESH
            )
        pl.semaphore_wait(barrier, N_TM - 1 + N_CLIP - 1)
        for i in range(1, N_TM):
            pl.semaphore_signal(ready, inc=1, device_id={"tm": i}, device_id_type=MESH)

    @pl.when(has_far)
    def _():
        pl.semaphore_wait(barrier, 2)

    @pl.when(me == N_TM - 1)
    def _():
        pl.semaphore_wait(barrier, 1)

    def transfer(side, a, g):
        source = qn_own if a == 3 else (k_hbm, v_hbm, g_hbm)[a].at[0]
        return pltpu.make_async_remote_copy(
            src_ref=source.at[:, packet_cols(g)],
            dst_ref=halo.at[side, a, :, packet_cols(g)],
            send_sem=send_sem.at[side, a, g],
            recv_sem=recv_sem.at[side, a, g],
            device_id={"tm": sides[side]},
            device_id_type=MESH,
        )

    def stat_transfer(side, g):
        return pltpu.make_async_remote_copy(
            src_ref=stat_mine.at[g],
            dst_ref=stat_halo.at[side, g],
            send_sem=stat_send.at[side, g],
            recv_sem=stat_recv.at[side, g],
            device_id={"tm": sides[side]},
            device_id_type=MESH,
        )

    def send_near(a):
        for g in range(PACKETS):
            transfer(0, a, g).start()

    def send_far(arrays, g):
        @pl.when(has_far)
        def _():
            for a in arrays:
                transfer(1, a, g).start()

    def receive_near(arrays, g):
        for a in arrays:
            transfer(0, a, g).wait_recv()

    def receive_far(arrays, g):
        @pl.when(has_far)
        def _():
            for a in arrays:
                transfer(1, a, g).wait_recv()

    for g in range(PACKETS):
        send_far((0, 1), g)
    for a in (0, 1, 2):
        send_near(a)

    @pl.when(jnp.logical_not(has_far))
    def _():
        halo[1] = jnp.zeros((4, TOK, HH), jnp.bfloat16)
        stat_halo[1] = jnp.zeros((GROUPS, 8, TOK), jnp.float32)

    for load in small:
        load.wait()
    rows = lax.broadcasted_iota(jnp.int32, (TOK, TOK), 0)
    lanes = lax.broadcasted_iota(jnp.int32, (TOK, TOK), 1)

    def window_of(where, position, present):
        chosen = jnp.zeros((TOK, TOK), jnp.int32)
        for t in range(GW):
            start = starts[0, position * GW + t]
            chosen = jnp.where(where // TILE == t, jnp.where(present, start, -100), chosen)
        return chosen

    def bias_of(window, keys, count):
        column = keys // TILE
        frame = (keys % TILE) // FRAME
        live = (column >= window) & (column < window + WW) & (frame < count)
        return jnp.where(live, 0.0, DEAD).astype(jnp.float32)

    known = jnp.where(has_far, far, me)
    mine = window_of(rows, me, me >= 0)
    count_own = frames[0, me]
    bias_f[0] = bias_of(mine, lanes, frames[0, near])
    bias_f[1] = bias_of(mine, lanes, count_own)
    bias_f[2] = bias_of(mine, lanes, jnp.where(has_far, frames[0, known], 0))
    bias_b[0] = bias_of(window_of(lanes, near, me >= 0), rows, count_own)
    bias_b[1] = bias_of(window_of(lanes, known, has_far), rows, count_own)

    gain_acc[...] = jnp.zeros_like(gain_acc)
    stat_cols[...] = jnp.zeros_like(stat_cols)
    gain_q = q_gain[...]
    gain_k = k_gain[...]
    ungain_k = 1.0 / gain_k
    for load in loads:
        load.wait()

    def normal_queries(h, carry):
        values = raw[0, :, cols(h)].astype(jnp.float32)
        qn_own[:, cols(h)] = (values * inv_rms(values) * gain_q).astype(jnp.bfloat16)
        return carry

    lax.fori_loop(0, H, normal_queries, 0)
    send_far((2, 3), 0)

    @pl.when(middle)
    def _():
        send_far((2,), 1)

    send_near(3)

    stat_lane = lax.broadcasted_iota(jnp.int32, (TOK, HD), 1)

    def forward_head(local, g):
        h = g * PER + local
        at = cols(h)
        qn = qn_own[:, at]
        grads = raw[3, :, at]
        keys, extras, values = [], [], []
        for p in range(3):
            rough = (halo[0, 0, :, at], raw[1, :, at], halo[1, 0, :, at])[p].astype(jnp.float32)
            hat = rough * inv_rms(rough)
            kn = (hat * gain_k).astype(jnp.bfloat16)
            keys.append(kn)
            extras.append((hat - kn.astype(jnp.float32) * ungain_k).astype(jnp.bfloat16))
            values.append((halo[0, 1, :, at], raw[2, :, at], halo[1, 1, :, at])[p])
        kn_own[:, at] = keys[1]
        scores = [dot(qn, keys[p], NT) * SCALE + bias_f[p] for p in range(3)]
        peak = jnp.max(jnp.maximum(jnp.maximum(scores[0], scores[1]), scores[2]), axis=-1, keepdims=True)
        weights = [jnp.exp2(s - peak) for s in scores]
        mass = jnp.sum(weights[0] + weights[1] + weights[2], axis=-1, keepdims=True)
        inverse = 1.0 / mass
        probs = [w * inverse for w in weights]
        slopes = [dot(grads, values[p], NT) for p in range(3)]
        delta = jnp.sum(
            probs[0] * slopes[0] + probs[1] * slopes[1] + probs[2] * slopes[2], axis=-1, keepdims=True
        )
        low = [x.astype(jnp.bfloat16) for x in probs]
        change = [(probs[p] * (slopes[p] - delta)).astype(jnp.bfloat16) for p in range(3)]
        stage[0, :, at] = sum(dot(low[p], values[p]) for p in range(3)).astype(jnp.bfloat16)
        wide = sum(
            dot(change[p], jnp.concatenate([keys[p], extras[p]], axis=1)) for p in range(3)
        )
        dqn = wide[:, :HD] * ROOT
        by_hat = dqn * ungain_k + wide[:, HD:] * ROOT
        query = raw[0, :, at].astype(jnp.float32)
        scale = inv_rms(query)
        gain_acc[0] += fold(dqn * query * scale)
        gain_acc[1] += fold(qn.astype(jnp.float32) * by_hat)
        stage[1, :, at] = norm_back(query, scale, gain_q, dqn).astype(jnp.bfloat16)
        acc[0, :, at] = dot(change[1], qn, TN)
        acc[1, :, at] = dot(low[1], grads, TN)
        logs = peak + jnp.log2(mass)
        kept = stat_cols[...]
        kept = jnp.where(stat_lane == 2 * local, logs, kept)
        stat_cols[...] = jnp.where(stat_lane == 2 * local + 1, delta, kept)
        return g

    def out_copy(ref, i, g):
        return pltpu.make_async_copy(
            stage.at[i, :, packet_cols(g)], ref.at[0, :, packet_cols(g)], out_sem.at[i, g]
        )

    def keep_stats(g):
        stat_mine[g] = jnp.transpose(stat_cols[...])[:8]
        stat_transfer(0, g).start()

        @pl.when(has_far)
        def _():
            stat_transfer(1, g).start()

    def forward_group(g, carry):
        receive_near((0, 1), g)
        receive_far((0, 1), g)
        lax.fori_loop(0, PER, forward_head, g, unroll=True)
        keep_stats(g)
        out_copy(att_out, 0, g).start()
        out_copy(dq_out, 1, g).start()
        return carry

    lax.fori_loop(0, FULL, forward_group, 0)
    for local in range(PER):
        receive_near((0, 1), FULL + local)
        receive_far((0, 1), FULL + local)
        forward_head(local, FULL)

    row8 = lax.broadcasted_iota(jnp.int32, (8, HD), 0)
    query_part = jnp.sum(gain_acc[0], axis=0, keepdims=True)
    key_part = jnp.sum(gain_acc[1], axis=0, keepdims=True)
    part[...] = jnp.where(row8 == 0, query_part, jnp.where(row8 == 1, key_part, 0.0))

    def to_ring(i):
        return pltpu.make_async_remote_copy(
            src_ref=part, dst_ref=ring_in.at[i], send_sem=ring_send, recv_sem=ring_recv.at[i],
            device_id={"tm": 0}, device_id_type=MESH,
        )

    @pl.when(me > 0)
    def _():
        pl.semaphore_wait(ready, 1)
        to_ring(me).start()

    keep_stats(FULL)

    @pl.when(jnp.logical_not(middle))
    def _():
        send_far((2,), 1)

    send_far((3,), 1)

    for g in range(2, PACKETS):
        send_far((3, 2), g)

    for n in range(FULL, PACKETS):
        out_copy(att_out, 0, n).start()
        out_copy(dq_out, 1, n).start()

    def to_clip(c, slot):
        return pltpu.make_async_remote_copy(
            src_ref=clip_in.at[clip], dst_ref=clip_in.at[slot], send_sem=clip_send.at[c],
            recv_sem=clip_recv.at[slot], device_id={"clip": c},
            device_id_type=MESH,
        )

    def to_all(i):
        return pltpu.make_async_remote_copy(
            src_ref=total, dst_ref=gains_out, send_sem=total_send.at[i], recv_sem=total_recv,
            device_id={"tm": i}, device_id_type=MESH,
        )

    @pl.when(me == 0)
    def _():
        ring = part[...]
        for i in range(1, N_TM):
            to_ring(i).wait_recv()
            ring = ring + ring_in[i]
        clip_in[clip] = ring
        for c in range(N_CLIP):

            @pl.when(clip != c)
            def _():
                to_clip(c, clip).start()

    def own_total():
        return pltpu.make_async_copy(total, gains_out, own_sem)

    def share_total():
        for c in range(N_CLIP):

            @pl.when(clip != c)
            def _():
                to_clip(c, c).wait_recv()

        everything = clip_in[0]
        for c in range(1, N_CLIP):
            everything = everything + clip_in[c]
        total[...] = everything
        for i in range(1, N_TM):
            to_all(i).start()
        own_total().start()

    def backward_terms(side, local, g, between=None):
        at = cols(g * PER + local)
        qn = halo[side, 3, :, at]
        logs = stat_halo[side, g, pl.ds(2 * local, 1), :]
        delta = stat_halo[side, g, pl.ds(2 * local + 1, 1), :]
        probs = jnp.exp2(dot(kn_own[:, at], qn, NT) * SCALE + bias_b[side] - logs)
        if between is not None:
            between()
        grads = halo[side, 2, :, at]
        slopes = dot(raw[2, :, at], grads, NT)
        change = (probs * (slopes - delta)).astype(jnp.bfloat16)
        return (
            acc[0, :, at] + dot(change, qn),
            acc[1, :, at] + dot(probs.astype(jnp.bfloat16), grads),
        )

    def near_head(local, g):
        at = cols(g * PER + local)
        dk, dv = backward_terms(0, local, g)
        acc[0, :, at] = dk
        acc[1, :, at] = dv
        return g

    def far_head(local, g, between=None):
        at = cols(g * PER + local)
        dk, dv = backward_terms(1, local, g, between)
        rough = raw[1, :, at].astype(jnp.float32)
        stage[2, :, at] = norm_back(rough, inv_rms(rough), gain_k, dk * ROOT).astype(jnp.bfloat16)
        stage[3, :, at] = dv.astype(jnp.bfloat16)
        return g

    def backward_group(g, carry):
        stat_transfer(0, g).wait_recv()
        receive_near((2, 3), g)
        lax.fori_loop(0, PER, near_head, g, unroll=True)

        @pl.when(has_far)
        def _():
            stat_transfer(1, g).wait_recv()

        receive_far((2, 3), g)

        lax.fori_loop(0, PER, far_head, g, unroll=True)
        out_copy(dk_out, 2, g).start()
        out_copy(dv_out, 3, g).start()
        return carry

    lax.fori_loop(0, FULL, backward_group, 0)
    stat_transfer(0, FULL).wait_recv()
    for local in range(PER):
        receive_near((2, 3), FULL + local)
        near_head(local, FULL)

    def all_sent(side, arrays):
        for n in range(PACKETS):
            for a in arrays:
                transfer(side, a, n).wait_send()

    all_sent(0, (0, 1, 2, 3))
    for g in range(GROUPS):
        stat_transfer(0, g).wait_send()

    @pl.when(has_far)
    def _():
        all_sent(1, (0, 1))
        for g in range(GROUPS):
            stat_transfer(1, g).wait_send()
        stat_transfer(1, FULL).wait_recv()

    @pl.when(me > 0)
    def _():
        to_ring(me).wait_send()

    for n in range(PACKETS):
        out_copy(att_out, 0, n).wait()
        out_copy(dq_out, 1, n).wait()
    for n in range(FULL):
        out_copy(dk_out, 2, n).wait()
        out_copy(dv_out, 3, n).wait()

    for local in range(PER):
        receive_far((3,), FULL + local)
        far_head(local, FULL, lambda: receive_far((2,), FULL + local))
        out_copy(dk_out, 2, FULL + local).start()
        out_copy(dv_out, 3, FULL + local).start()

    @pl.when(me == 0)
    def _():
        share_total()

    @pl.when(has_far)
    def _():
        all_sent(1, (2, 3))

    for n in range(FULL, PACKETS):
        out_copy(dk_out, 2, n).wait()
        out_copy(dv_out, 3, n).wait()

    @pl.when(me == 0)
    def _():
        for c in range(N_CLIP):

            @pl.when(clip != c)
            def _():
                to_clip(c, clip).wait_send()

        for i in range(1, N_TM):
            to_all(i).wait_send()
        own_total().wait()

    @pl.when(me > 0)
    def _():
        to_all(0).wait_recv()


def finish_kernel(*refs):
    ins, gains, outs, q_total, k_total = refs[:4], refs[4], refs[5:9], refs[9], refs[10]
    out_sem = refs[11]
    writes = [pltpu.make_async_copy(ins[i], outs[i], out_sem.at[i]) for i in range(4)]
    for write in writes:
        write.start()
    q_total[...] = gains[0:1]
    k_total[...] = gains[1:2]
    for write in writes:
        write.wait()


def on_device(
    queries, key_rows, value_rows, grad_out, query_gain, key_gain, valid_frames, window_start
):
    any_spec = pl.BlockSpec(memory_space=pl.ANY)
    vmem_spec = pl.BlockSpec(memory_space=pltpu.VMEM)
    slab = jax.ShapeDtypeStruct((1, TOK, HH), jnp.bfloat16)
    dma = pltpu.SemaphoreType.DMA
    bf16, f32 = jnp.bfloat16, jnp.float32
    results = pl.pallas_call(
        main_kernel,
        out_shape=[slab] * 4 + [jax.ShapeDtypeStruct((8, HD), f32)],
        in_specs=[any_spec] * 8,
        out_specs=[any_spec] * 5,
        scratch_shapes=[
            pltpu.VMEM((1, HD), f32),
            pltpu.VMEM((1, HD), f32),
            pltpu.SMEM((1, N_TM), jnp.int32),
            pltpu.SMEM((1, N_TM * GW), jnp.int32),
            pltpu.VMEM((4, TOK, HH), bf16),
            pltpu.VMEM((2, 4, TOK, HH), bf16),
            pltpu.VMEM((TOK, HH), bf16),
            pltpu.VMEM((TOK, HH), bf16),
            pltpu.VMEM((2, TOK, HH), f32),
            pltpu.VMEM((4, TOK, HH), bf16),
            pltpu.VMEM((3, TOK, TOK), f32),
            pltpu.VMEM((2, TOK, TOK), f32),
            pltpu.VMEM((TOK, HD), f32),
            pltpu.VMEM((GROUPS, 8, TOK), f32),
            pltpu.VMEM((2, GROUPS, 8, TOK), f32),
            pltpu.VMEM((2, 8, HD), f32),
            pltpu.VMEM((8, HD), f32),
            pltpu.VMEM((N_TM, 8, HD), f32),
            pltpu.VMEM((N_CLIP, 8, HD), f32),
            pltpu.VMEM((8, HD), f32),
            dma((4,)),
            dma((4,)),
            dma((4, PACKETS)),
            dma((2, 4, PACKETS)),
            dma((2, 4, PACKETS)),
            dma((2, GROUPS)),
            dma((2, GROUPS)),
            pltpu.SemaphoreType.REGULAR,
            dma,
            dma((N_TM,)),
            dma((N_CLIP,)),
            dma((N_CLIP,)),
            dma((N_TM,)),
            dma,
            dma,
        ],
        compiler_params=pltpu.CompilerParams(
            collective_id=0, has_side_effects=True, vmem_limit_bytes=203 * 2**18
        ),
        name="attend",
    )(
        queries, key_rows, value_rows, grad_out,
        query_gain.reshape(1, HD), key_gain.reshape(1, HD), valid_frames, window_start,
    )
    row = jax.ShapeDtypeStruct((1, HD), f32)
    outs = pl.pallas_call(
        finish_kernel,
        out_shape=[slab] * 4 + [row] * 2,
        in_specs=[vmem_spec] * 5,
        out_specs=[any_spec] * 4 + [vmem_spec] * 2,
        scratch_shapes=[dma((4,))],
        compiler_params=pltpu.CompilerParams(vmem_limit_bytes=8 * 2**20),
        name="finish",
    )(*results)
    return (*outs[:4], outs[4].reshape(HD), outs[5].reshape(HD))


def solution(mesh):
    slabs = P("clip", "tm", None)
    return jax.shard_map(
        on_device,
        mesh=mesh,
        in_specs=(slabs,) * 4 + (P(), P(), P("clip", None), P("clip", None)),
        out_specs=(slabs,) * 4 + (P(), P()),
        check_vma=False,
    )
```
